32 devices in a mesh: seq: 4 (over z), exp: 4 (over x, core), dp: 2 (over y).
Axes of the slice: x: 2, y: 2, z: 4, core: 2. Of those that a mesh axis runs over, the one named last changes fastest.
Arguments:
- queries: bfloat16 [768, 24, 128], P(('dp', 'seq'), 'exp'), parts along dimension 0, may hold values from -4.5 to 4.5
- keys: bfloat16 [768, 4, 128], P(('dp', 'seq'), 'exp'), parts along dimension 0, may hold values from -4.5 to 4.5
- values: bfloat16 [768, 4, 128], P(('dp', 'seq'), 'exp'), parts along dimension 0, may hold values from -16 to 16
- doc_ids: int32 [768], P('dp'), parts along dimension 0, may hold values from 0 to 2, never falling along the last dimension, each value on 1 to 320 neighbouring positions
- norm_gain: float32 [3072], replicated, may hold values from 0.1 to 1.9
- expert_ids: int32 [768, 2], P(('dp', 'seq', 'exp')), parts along dimension 0, may hold values from 0 to 3, all different within a row; in each aligned block of 24 rows (0 to 23, 24 to 47, ...) at most 12 rows name the same one
- route_weights: float32 [768, 2], P(('dp', 'seq', 'exp')), parts along dimension 0, may hold values from 0.2 to 1
- w_in: bfloat16 [4, 3072, 2048], P('exp', None, 'seq'), may hold values from -0.109375 to 0.109375
- w_out: bfloat16 [4, 2048, 3072], P('exp', 'seq'), may hold values from -0.125 to 0.125
Outputs:
- mixed: bfloat16 [768, 3072], P(('dp', 'seq', 'exp')), parts along dimension 0
The draws below stay inside these ranges and needn't reach their ends.
There are 2 independent parts, one for each index of `dp`. The reference program is written for one: setup_inputs(seed, part) draws one part's arguments, and reference() takes and returns one part's arrays. A program takes and returns all parts, laid end to end along the dimension named above; an argument that names none is the same for every part. Nothing has to cross between parts.
Inputs may be any that keep to these rules, and one draw needn't show every extreme that they name: `doc_ids`: never falling along the sequence. `expert_ids`: within the 24 tokens of one device no expert is named by more than 12 tokens, and in every draw some expert of some device is named by exactly 12; the two experts of a token differ.
All inputs are finite; a program needn't handle non-finite values.
Results may differ from the reference program's by a relative error of at most 0.015.
Values may be sent and summed in bfloat16 or wider, within the bound.
No kernel may reach another device: no remote copies, remote signals or barrier semaphores. Data moves between devices by JAX's collectives and lax.ppermute only.
A program may use at most 128 MiB of HBM per device.

```python
import math
import jax
import jax.numpy as jnp
import numpy as np
from jax import lax

HEAD = 128
QH_DEV = 6
HEADS = 24
KV_HEADS = 4
D = 3072
EXPERTS = 4
FF_DEV = 512
FFW = 2048
TOK = 24
SEQ_BLK = 96
TOKENS = 384
CAP = 12
WINDOW = 2048
NDOC = 3
N_SEQ = 4


def draw_keys(key, part):
    drawn = jnp.clip(jax.random.normal(jax.random.fold_in(key, 3), (TOKENS, KV_HEADS, HEAD), jnp.float32), -4.5, 4.5)
    return drawn.astype(jnp.bfloat16)


def draw_queries(key, part):
    drawn = jnp.clip(jax.random.normal(jax.random.fold_in(key, 5), (TOKENS, HEADS, HEAD), jnp.float32), -4.5, 4.5)
    return drawn.astype(jnp.bfloat16)


def level_of(key, dims, pieces, least, high):
    def one(dim, shards_of):
        draws = jax.random.uniform(jax.random.fold_in(jax.random.fold_in(key, 6), dim), (shards_of,), jnp.float32, least / len(pieces), high / len(pieces))
        return jnp.repeat(jnp.exp(draws), dims[dim] // shards_of).reshape((-1,) + (1,) * (len(dims) - dim - 1))

    loudness = one(*pieces[0])
    for cut in pieces[1:]:
        loudness = loudness * one(*cut)
    return loudness


def profile(count, total, reach, slope):
    loads = [(1 << 20) // math.isqrt(standing ** slope) + 1 for standing in range(2, count + 1)]
    rest, holding = total - reach - (count - 1), [1] * (count - 1)
    while rest > 0:
        candidates = [i for i in range(count - 1) if holding[i] < reach]
        mass, budget = sum([loads[i] for i in candidates]), rest
        for i in candidates:
            more = min(reach - holding[i], max(1, budget * loads[i] // mass), rest)
            holding[i] = holding[i] + more
            rest = rest - more
    return np.array([reach] + holding)


def uneven(key, number_of, total, reach, skew):
    if number_of == 2:
        one = jax.random.randint(key, (), max(1, total - reach), min(reach, total - 1) + 1)
        return jnp.stack([one, total - one])
    sizes = jnp.asarray(profile(number_of, total, reach, skew), jnp.int32)
    couples = (number_of - 1) // 2
    giver, sink = sizes[1:1 + 2 * couples:2], sizes[2:2 + 2 * couples:2]
    slack = jnp.minimum(giver - 1, reach - sink)
    passed = jax.random.randint(jax.random.fold_in(key, 1), (couples,), 0, 1 << 20) % (slack + 1)
    sizes = sizes.at[1:1 + 2 * couples:2].set(giver - passed).at[2:2 + 2 * couples:2].set(sink + passed)
    return sizes[jax.random.permutation(jax.random.fold_in(key, 2), number_of)]


def routed_block(key, own, number, rows, amount, top, bound, skew):
    ranking = jax.random.permutation(key, amount)
    heavy_load, common = load_shares(amount, rows * top, bound, skew, True), load_shares(amount, rows * top, bound, skew, False)
    places = jnp.arange(amount)

    def named(lengths, turn):
        used = int((lengths > 0).sum())
        fixed = max(1, used // 4)
        shifted = fixed + (places - fixed + turn * (used - fixed)) % max(1, amount - fixed)
        return jnp.zeros((amount,), jnp.int32).at[ranking[jnp.where(places < fixed, places, shifted)]].set(jnp.asarray(lengths, jnp.int32))

    lengths = jnp.where(number % 4 == 0, named(heavy_load, number // 4), named(common, number - number // 4 - 1))
    mixed = jax.random.permutation(jax.random.fold_in(own, 3), amount)
    donor, sink = mixed[0:amount // 2 * 2:2], mixed[1:amount // 2 * 2:2]
    slack = jnp.minimum(lengths[donor] - 1, bound - lengths[sink]) // 2
    slack = jnp.where((donor == ranking[0]) | (sink == ranking[0]) | (lengths[sink] == 0), 0, jnp.maximum(slack, 0))
    shifted = jax.random.randint(jax.random.fold_in(own, 4), (amount // 2,), 0, 1 << 20) % (slack + 1)
    lengths = lengths.at[donor].add(-shifted).at[sink].add(shifted)
    labels = jnp.searchsorted(jnp.cumsum(lengths), jnp.arange(rows * top), side="right").astype(jnp.int32)
    listing = labels.reshape(top, rows).T
    listing = listing[jax.random.permutation(jax.random.fold_in(own, 1), rows)]
    turn = jax.random.randint(jax.random.fold_in(own, 2), (rows, 1), 0, top)
    return jnp.take_along_axis(listing, (jnp.arange(top)[None, :] + turn) % top, axis=1)


def load_shares(count, total, bound, slope, full):
    portions = [(1 << 20) // math.isqrt(standing ** slope) + 1 for standing in range(1, count + 1)]
    largest = bound if full else min(bound, max(-(-total // count), total * portions[0] // sum(portions)))
    least = 1 if total - largest >= count - 1 else 0
    counts, surplus = [largest] + [least] * (count - 1), total - largest - least * (count - 1)
    while surplus > 0:
        free = [i for i in range(1, count) if counts[i] < largest] or [i for i in range(1, count) if counts[i] < bound]
        pool, remaining = sum([portions[i] for i in free]), surplus
        for i in free:
            more = min(bound - counts[i], max(1, remaining * portions[i] // pool), surplus)
            counts[i] = counts[i] + more
            surplus = surplus - more
    return np.array(counts)


def gaussian(key, shape, spread, limit, split=(), kind=jnp.bfloat16):
    factor_of = level_of(key, shape, split, -0.22, 0.18) if split else 1.0
    result = jax.random.normal(key, shape, jnp.float32) * spread * factor_of
    return jnp.minimum(jnp.maximum(result, -limit), limit).astype(kind)


def setup_inputs(seed: int = 0, part: int = 0) -> dict:
    streams_of = jax.random.split(jax.random.key(seed), 10)
    own_keys = jax.random.split(jax.random.fold_in(streams_of[9], part), 10)
    queries = draw_queries(jax.random.fold_in(jax.random.fold_in(streams_of[9], part), 71), part)
    keys = draw_keys(jax.random.fold_in(jax.random.fold_in(streams_of[9], part), 71), part)
    values = gaussian(own_keys[2], (TOKENS, KV_HEADS, HEAD), 4.0, 16.0, ((0, 4), (1, 4)))
    doc_ids = jnp.searchsorted(jnp.cumsum(uneven(own_keys[3], NDOC, TOKENS, TOKENS * 5 // 6, 0)), jnp.arange(TOKENS), side="right").astype(jnp.int32)
    norm_gain = jnp.clip(1.0 + 0.18 * jax.random.normal(streams_of[4], (D,), jnp.float32), 0.1, 1.9)
    expert_ids_keys = jax.random.split(jax.random.fold_in(own_keys[5], 1), TOKENS // TOK)
    expert_ids_turns = jax.random.permutation(jax.random.fold_in(own_keys[5], 3), TOKENS // TOK)
    expert_ids = jax.vmap(lambda own, number: routed_block(jax.random.fold_in(own_keys[5], 2), own, number, TOK, EXPERTS, 2, CAP, 2))(expert_ids_keys, expert_ids_turns).reshape((TOKENS, 2))
    route_weights = jnp.clip(0.2 + 0.8 * jax.random.uniform(own_keys[6], (TOKENS, 2), jnp.float32) ** level_of(own_keys[6], (TOKENS, 2), ((0, 16),), -0.2, 0.2), 0.2, 1.0)
    w_in = gaussian(streams_of[7], (EXPERTS, D, FFW), D ** -0.5, 0.109375, ((0, 4), (2, 4)))
    w_out = gaussian(streams_of[8], (EXPERTS, FFW, D), FFW ** -0.5, 0.125, ((0, 4), (1, 4)))
    return {"queries": queries, "keys": keys, "values": values, "doc_ids": doc_ids, "norm_gain": norm_gain, "expert_ids": expert_ids, "route_weights": route_weights, "w_in": w_in, "w_out": w_out}


epsilon = 1e-05

def attend_block(block_index, queries, keys, values, doc_ids):
    start = block_index * SEQ_BLK
    query_block = lax.dynamic_slice_in_dim(queries, start, SEQ_BLK, 0).astype(jnp.float32)
    query_block = query_block.reshape(SEQ_BLK, KV_HEADS, QH_DEV, HEAD)
    key_float = keys.astype(jnp.float32)
    value_float = values.astype(jnp.float32)
    score = jnp.einsum('bgqe,tge->gqbt', query_block, key_float) * (1.0 / HEAD ** 0.5)
    query_pos = start + jnp.arange(SEQ_BLK, dtype=jnp.int32)
    key_pos = jnp.arange(TOKENS, dtype=jnp.int32)
    query_doc = lax.dynamic_slice_in_dim(doc_ids, start, SEQ_BLK, 0)
    allowed = (key_pos[None, :] <= query_pos[:, None]) & (query_pos[:, None] - key_pos[None, :] < WINDOW)
    allowed = allowed & (query_doc[:, None] == doc_ids[None, :])
    score = jnp.where(allowed[None, None], score, -jnp.inf)
    top_score = lax.optimization_barrier(jnp.max(score, axis=3, keepdims=True))
    weights = jnp.where(allowed[None, None], jnp.exp(score - top_score), 0.0)
    probs = (weights / lax.optimization_barrier(jnp.sum(weights, axis=3, keepdims=True))).astype(jnp.bfloat16)
    output = jnp.einsum('gqbt,tge->bgqe', probs.astype(jnp.float32), value_float)
    return output.reshape(SEQ_BLK, D).astype(jnp.bfloat16)

def reference(queries, keys, values, doc_ids, norm_gain, expert_ids, route_weights, w_in, w_out):
    attn = lax.map(lambda index: attend_block(index, queries, keys, values, doc_ids), jnp.arange(N_SEQ, dtype=jnp.int32))
    attn = attn.reshape(TOKENS, D)
    attn_float = attn.astype(jnp.float32)
    mean_square = lax.optimization_barrier(jnp.mean(attn_float * attn_float, axis=1, keepdims=True))
    normed = (attn_float * lax.rsqrt(mean_square + epsilon) * norm_gain[None, :]).astype(jnp.bfloat16)
    run_count = TOKENS // TOK
    flat_ids = expert_ids.reshape(run_count, TOK * 2)
    onehot = (flat_ids[:, :, None] == jnp.arange(EXPERTS, dtype=jnp.int32)[None, None, :]).astype(jnp.int32)
    earlier = jnp.cumsum(onehot, axis=1) - onehot
    slot = lax.optimization_barrier(jnp.sum(earlier * onehot, axis=2))
    row_code = (jnp.arange(run_count, dtype=jnp.int32)[:, None] * CAP + slot).reshape(TOKENS, 2)
    token_code = jnp.arange(TOKENS, dtype=jnp.int32)[:, None] + jnp.zeros((1, 2), jnp.int32)
    table = jnp.zeros((EXPERTS, run_count * CAP), jnp.int32).at[expert_ids, row_code].set(token_code + 1)
    padded = jnp.concatenate([jnp.zeros((1, D), jnp.bfloat16), normed], axis=0)

    def run_expert(expert):
        rows = padded[table[expert]]
        hidden = jax.nn.silu(jnp.dot(rows, w_in[expert], preferred_element_type=jnp.float32)).astype(jnp.bfloat16)
        out_weight = w_out[expert]

        def add_slice(total, index):
            hidden_part = lax.dynamic_slice_in_dim(hidden, index * FF_DEV, FF_DEV, 1)
            weight_part = lax.dynamic_slice_in_dim(out_weight, index * FF_DEV, FF_DEV, 0)
            partial_value = jnp.dot(hidden_part, weight_part, preferred_element_type=jnp.float32).astype(jnp.bfloat16)
            partial_value = lax.optimization_barrier(partial_value)
            return (total + partial_value.astype(jnp.float32), None)
        total, unused = lax.scan(add_slice, jnp.zeros((run_count * CAP, D), jnp.float32), jnp.arange(N_SEQ, dtype=jnp.int32))
        return total.astype(jnp.bfloat16)
    expert_out = lax.map(run_expert, jnp.arange(EXPERTS, dtype=jnp.int32))
    picked = expert_out[expert_ids, row_code].astype(jnp.float32)
    mixed = attn_float + route_weights[:, 0:1] * picked[:, 0] + route_weights[:, 1:2] * picked[:, 1]
    return mixed.astype(jnp.bfloat16)
```

```python
import functools

import jax
import jax.numpy as jnp
from jax import lax
from jax.experimental import pallas as pl
from jax.experimental.pallas import tpu as pltpu
from jax.sharding import PartitionSpec as P

WINDOW = 2048


epsilon = 1e-05


def shifted(x, axis, by):
    size = lax.axis_size(axis)
    pairs = [(i, i + by) for i in range(size) if 0 <= i + by < size]
    return lax.ppermute(x, axis, pairs)


def flipped(x, axis, by):
    return lax.ppermute(x, axis, [(i, i ^ by) for i in range(lax.axis_size(axis))])


def routed_shards(
    queries, keys, values, doc_ids, norm_gain, expert_ids, route_weights, w_in, w_out
):
    block_len, heads_dev, head_dim = queries.shape
    seq_count = lax.axis_size("seq")
    exp_count = lax.axis_size("exp")
    seq_index = lax.axis_index("seq")
    reach_blocks = min(-(-WINDOW // block_len), seq_count - 1)
    own_keys = keys[:, 0, :]
    own_values = values[:, 0, :]
    key_list = [own_keys]
    value_list = [own_values]
    for distance in range(1, reach_blocks + 1):
        far_keys, far_values = shifted((own_keys, own_values), "seq", distance)
        key_list.insert(0, far_keys)
        value_list.insert(0, far_values)
    near_keys = jnp.concatenate(key_list, axis=0)
    near_values = jnp.concatenate(value_list, axis=0)
    key_count = near_keys.shape[0]
    query_rows = jnp.transpose(queries, (1, 0, 2)).reshape(heads_dev * block_len, head_dim)
    score = lax.dot_general(
        query_rows, near_keys, (((1,), (1,)), ((), ())), preferred_element_type=jnp.float32
    )
    score = score * (1.0 / head_dim**0.5)
    query_pos = seq_index * block_len + jnp.arange(block_len, dtype=jnp.int32)
    key_pos = (seq_index - reach_blocks) * block_len + jnp.arange(key_count, dtype=jnp.int32)
    padded_docs = jnp.concatenate(
        [jnp.full((reach_blocks * block_len,), -1, jnp.int32), doc_ids], axis=0
    )
    key_docs = lax.dynamic_slice_in_dim(padded_docs, seq_index * block_len, key_count, 0)
    query_docs = lax.dynamic_slice_in_dim(doc_ids, seq_index * block_len, block_len, 0)
    allowed = (key_pos[None, :] <= query_pos[:, None]) & (
        query_pos[:, None] - key_pos[None, :] < WINDOW
    )
    allowed = allowed & (key_pos[None, :] >= 0) & (query_docs[:, None] == key_docs[None, :])
    allowed = jnp.tile(allowed, (heads_dev, 1))
    score = jnp.where(allowed, score, -jnp.inf)
    top_score = jnp.max(score, axis=1, keepdims=True)
    weights = jnp.where(allowed, jnp.exp(score - top_score), 0.0)
    probs = (weights / jnp.sum(weights, axis=1, keepdims=True)).astype(jnp.bfloat16)
    attended = jnp.dot(probs, near_values, preferred_element_type=jnp.float32).astype(jnp.bfloat16)
    attended = jnp.transpose(attended.reshape(heads_dev, block_len, head_dim), (1, 0, 2)).reshape(
        block_len, heads_dev * head_dim
    )
    attn = lax.all_to_all(attended, "exp", split_axis=0, concat_axis=1, tiled=True)
    token_count = attn.shape[0]
    width = attn.shape[1]
    attn_float = attn.astype(jnp.float32)
    mean_square = jnp.mean(attn_float * attn_float, axis=1, keepdims=True)
    normed = (attn_float * lax.rsqrt(mean_square + epsilon) * norm_gain[None, :]).astype(
        jnp.bfloat16
    )
    capacity = max((token_count + 2) // 3, 2 * token_count // exp_count)
    flat_ids = expert_ids.reshape(token_count * 2)
    onehot = (flat_ids[:, None] == jnp.arange(exp_count, dtype=jnp.int32)[None, :]).astype(
        jnp.int32
    )
    earlier = jnp.cumsum(onehot, axis=0) - onehot
    slot = jnp.sum(earlier * onehot, axis=1)
    local_code = (flat_ids * capacity + slot).reshape(token_count, 2)
    slot_range = jnp.arange(exp_count * capacity, dtype=jnp.int32)
    first_hit = local_code[:, 0:1] == slot_range[None, :]
    second_hit = local_code[:, 1:2] == slot_range[None, :]
    placing = jnp.transpose((first_hit | second_hit).astype(jnp.bfloat16))
    outgoing = jnp.dot(placing, normed, preferred_element_type=jnp.float32).astype(jnp.bfloat16)
    arrived = lax.all_to_all(
        outgoing.reshape(exp_count, capacity, width), "exp", split_axis=0, concat_axis=0, tiled=True
    )
    row_count = exp_count * capacity
    arrived = arrived.reshape(row_count, width)
    weight_in = w_in[0]
    weight_out = w_out[0]
    hidden = jax.nn.silu(
        jnp.dot(
            lax.all_gather(arrived, "seq", axis=0, tiled=True),
            weight_in,
            preferred_element_type=jnp.float32,
        )
    ).astype(jnp.bfloat16)
    summed = lax.psum_scatter(
        jnp.dot(hidden, weight_out, preferred_element_type=jnp.float32).astype(jnp.bfloat16),
        "seq",
        scatter_dimension=0,
        tiled=True,
    )
    expert_out = summed.reshape(exp_count, capacity, width)
    returned = lax.all_to_all(expert_out, "exp", split_axis=0, concat_axis=0, tiled=True).reshape(
        row_count, width
    )
    combine = route_weights[:, 0:1] * first_hit.astype(jnp.float32) + route_weights[
        :, 1:2
    ] * second_hit.astype(jnp.float32)
    moe_part = jnp.dot(
        combine,
        returned.astype(jnp.float32),
        precision=lax.Precision.HIGHEST,
        preferred_element_type=jnp.float32,
    )
    return (attn_float + moe_part).astype(jnp.bfloat16)


def attend_kernel(block_len, scale, *refs):
    count = len(refs) - 6
    query_ref, packs = refs[0], refs[1 : 1 + count]
    query_info, key_info, out_ref, keys_ref, values_ref = refs[1 + count :]
    for i, pack in enumerate(packs):
        rows = slice(i * block_len, (i + 1) * block_len)
        keys_ref[rows] = pack[0:block_len]
        values_ref[rows] = pack[block_len : 2 * block_len]
    query_pos, query_doc = query_info[:, 0:1], query_info[:, 1:2]
    key_pos, key_doc = key_info[0:1, :], key_info[1:2, :]
    allowed = (key_pos <= query_pos) & (query_pos - key_pos < WINDOW) & (query_doc == key_doc)
    head_dim = query_ref.shape[2]
    for head in range(query_ref.shape[0]):
        score = lax.dot_general(
            query_ref[head],
            keys_ref[...],
            (((1,), (1,)), ((), ())),
            preferred_element_type=jnp.float32,
        )
        score = jnp.where(allowed, score * scale, -jnp.inf)
        weights = jnp.exp(score - jnp.max(score, axis=1, keepdims=True))
        probs = weights * (1.0 / jnp.sum(weights, axis=1, keepdims=True))
        out_ref[:, head * head_dim : (head + 1) * head_dim] = jnp.dot(
            probs.astype(jnp.bfloat16), values_ref[...], preferred_element_type=jnp.float32
        ).astype(jnp.bfloat16)


def experts_kernel(seq_count, exp_count, order, *refs):
    place_ref, weight_ref, gain_ref, w_in_ref, w_out_ref = refs[:5]
    blocks = refs[5 : 5 + seq_count * exp_count]
    outs = refs[5 + seq_count * exp_count : -2]
    kept, sent, own_ref = outs[:seq_count], outs[seq_count : 2 * seq_count], outs[-1]
    hidden_ref, split_ref = refs[-2:]
    place = place_ref[0]
    block_len, part_width = blocks[0].shape
    token_count = block_len // exp_count
    width = part_width * exp_count
    inverse = []
    for d in range(seq_count):
        total = jnp.zeros((block_len, 1), jnp.float32)
        for j in range(exp_count):
            value = blocks[d * exp_count + j][...].astype(jnp.float32)
            total = total + jnp.sum(value * value, axis=1, keepdims=True)
        inverse.append(lax.rsqrt(total * (1.0 / width) + epsilon))
    hidden = None
    for j in range(exp_count):
        source = place ^ j
        gain = gain_ref[source]
        normed = []
        for d in range(seq_count):
            value = blocks[d * exp_count + j][...].astype(jnp.float32)
            normed.append((value * inverse[d] * gain).astype(jnp.bfloat16))
            if d == 0:
                split_ref[...] = value.reshape(exp_count, token_count, part_width)
                own_ref[source] = split_ref[place].astype(jnp.bfloat16)
        rows = pl.ds(pl.multiple_of(source * part_width, part_width), part_width)
        product = jnp.dot(
            jnp.concatenate(normed, axis=0), w_in_ref[rows, :], preferred_element_type=jnp.float32
        )
        hidden = product if hidden is None else hidden + product
    hidden = hidden * (1.0 / (1.0 + jnp.exp(-hidden)))
    hidden_ref[...] = hidden.reshape(seq_count * exp_count, token_count, hidden.shape[1])
    hidden = jnp.concatenate(
        [hidden_ref[d * exp_count + (place ^ j)] for d in range(seq_count) for j in order], axis=0
    ).astype(jnp.bfloat16)
    half = block_len // 2
    tile = part_width
    weight = weight_ref[...]
    for start in range(0, width, tile):
        columns = slice(start, start + tile)
        product = jnp.dot(hidden, w_out_ref[:, columns], preferred_element_type=jnp.float32)
        product = (product * weight).astype(jnp.bfloat16)
        for d in range(seq_count):
            low = d * block_len
            kept[d][:, columns] = product[low : low + half]
            sent[d][:, columns] = product[low + half : low + block_len]


def vmem():
    return pl.BlockSpec(memory_space=pltpu.VMEM)


def gathered_shards(
    queries, keys, values, doc_ids, norm_gain, expert_ids, route_weights, w_in, w_out
):
    block_len, heads_dev, head_dim = queries.shape
    seq_count = lax.axis_size("seq")
    exp_count = lax.axis_size("exp")
    seq_index = lax.axis_index("seq")
    exp_index = lax.axis_index("exp")
    token_count = expert_ids.shape[0]
    part_width = heads_dev * head_dim
    width = part_width * exp_count
    hidden_width = w_in.shape[2]
    half = block_len // 2
    far = range(1, seq_count)

    named = expert_ids[:, :, None] == jnp.arange(exp_count, dtype=jnp.int32)[None, None, :]
    dense = jnp.sum(jnp.where(named, route_weights[:, :, None], 0.0), axis=1).T
    pieces = []
    for _ in range(3):
        piece = lax.reduce_precision(dense, 8, 7)
        pieces.append(piece.astype(jnp.bfloat16))
        dense = dense - piece
    pieces = jnp.concatenate(pieces, axis=0)
    pieces = jnp.pad(pieces, ((0, 16 - 3 * exp_count), (0, head_dim - token_count)))

    pack = jnp.concatenate([keys[:, 0, :], values[:, 0, :], pieces], axis=0)
    packs = [pack] + [flipped(pack, "seq", d) for d in far]

    blocks_docs = doc_ids.reshape(seq_count, block_len)
    block_of = seq_index ^ jnp.arange(seq_count, dtype=jnp.int32)
    offsets = jnp.arange(block_len, dtype=jnp.int32)
    key_pos = (block_of[:, None] * block_len + offsets[None, :]).reshape(-1)
    key_docs = jnp.concatenate(
        [lax.dynamic_slice_in_dim(doc_ids, (seq_index ^ d) * block_len, block_len, 0) for d in range(seq_count)]
    )
    key_info = jnp.stack([key_pos, key_docs])
    query_info = jnp.stack([key_pos[:block_len], key_docs[:block_len]], axis=1)
    attended = pl.pallas_call(
        functools.partial(attend_kernel, block_len, 1.0 / head_dim**0.5),
        out_shape=jax.ShapeDtypeStruct((block_len, part_width), jnp.bfloat16),
        in_specs=[vmem()] * (seq_count + 3),
        out_specs=vmem(),
        scratch_shapes=[pltpu.VMEM((seq_count * block_len, head_dim), jnp.bfloat16)] * 2,
        cost_estimate=pl.CostEstimate(
            flops=4 * heads_dev * block_len * seq_count * block_len * head_dim,
            bytes_accessed=1 << 20,
            transcendentals=heads_dev * block_len * seq_count * block_len,
        ),
        name="attend",
    )(jnp.transpose(queries, (1, 0, 2)), *packs, query_info, key_info)

    blocks = {(d, 0): attended if d == 0 else flipped(attended, "seq", d) for d in range(seq_count)}
    shares = {0: jnp.stack([p[2 * block_len :] for p in packs])}
    bit = exp_count // 2
    while bit:
        blocks |= {(d, j ^ bit): flipped(block, "exp", bit) for (d, j), block in blocks.items()}
        held = sorted(shares)
        arrived = flipped(jnp.stack([shares[j] for j in held]), "exp", bit)
        shares |= {j ^ bit: arrived[i] for i, j in enumerate(held)}
        bit //= 2

    order = [j for j in range(exp_count) if not j & 1] + [j for j in range(exp_count) if j & 1]
    share = jnp.stack([shares[j] for j in order], axis=1)
    share = share.reshape(seq_count * exp_count, 16, head_dim)
    share = share[:, : 3 * exp_count, :token_count].reshape(-1, 3, exp_count, token_count)
    mine = jnp.arange(exp_count, dtype=jnp.int32) == exp_index
    weight = jnp.sum(
        jnp.where(mine[None, None, :, None], share.astype(jnp.float32), 0.0), axis=(1, 2)
    ).reshape(-1, 1)

    *returned, own = pl.pallas_call(
        functools.partial(experts_kernel, seq_count, exp_count, order),
        out_shape=[jax.ShapeDtypeStruct((half, width), jnp.bfloat16)] * (2 * seq_count)
        + [jax.ShapeDtypeStruct((exp_count, token_count, part_width), jnp.bfloat16)],
        in_specs=[pl.BlockSpec(memory_space=pltpu.SMEM)] + [vmem()] * (4 + seq_count * exp_count),
        out_specs=[vmem()] * (2 * seq_count + 1),
        scratch_shapes=[
            pltpu.VMEM((seq_count * exp_count, token_count, hidden_width), jnp.float32),
            pltpu.VMEM((exp_count, token_count, part_width), jnp.float32),
        ],
        compiler_params=pltpu.CompilerParams(vmem_limit_bytes=48 << 20),
        cost_estimate=pl.CostEstimate(
            flops=4 * seq_count * block_len * width * hidden_width,
            bytes_accessed=16 << 20,
            transcendentals=seq_count * block_len * hidden_width,
        ),
        name="experts",
    )(
        exp_index.reshape(1),
        weight,
        norm_gain.reshape(exp_count, 1, part_width),
        w_in[0],
        w_out[0],
        *[blocks[d, j] for d in range(seq_count) for j in range(exp_count)],
    )

    kept, sent = returned[:seq_count], returned[seq_count:]
    total = jnp.transpose(own, (1, 0, 2)).reshape(token_count, width).astype(jnp.float32)
    for d in reversed(range(seq_count)):
        both = kept[d].astype(jnp.float32) + flipped(sent[d], "exp", 1).astype(jnp.float32)
        away = flipped(both[token_count:].astype(jnp.bfloat16), "exp", 2)
        mine = both[:token_count] + away.astype(jnp.float32)
        if d:
            mine = flipped(mine.astype(jnp.bfloat16), "seq", d).astype(jnp.float32)
        total = total + mine
    return total.astype(jnp.bfloat16)


def solution(mesh):
    placed = (
        P(("dp", "seq"), "exp", None),
        P(("dp", "seq"), "exp", None),
        P(("dp", "seq"), "exp", None),
        P("dp"),
        P(),
        P(("dp", "seq", "exp"), None),
        P(("dp", "seq", "exp"), None),
        P("exp", None, "seq"),
        P("exp", "seq", None),
    )
    small = mesh.shape["seq"] == 4 and mesh.shape["exp"] == 4
    return jax.shard_map(
        gathered_shards if small else routed_shards,
        mesh=mesh,
        in_specs=placed,
        out_specs=P(("dp", "seq", "exp"), None),
        check_vma=False,
    )
```

```python
import functools

import jax
import jax.numpy as jnp
from jax import lax
from jax.experimental import pallas as pl
from jax.experimental.pallas import tpu as pltpu
from jax.sharding import PartitionSpec as P

WINDOW = 2048


epsilon = 1e-05


def shifted(x, axis, by):
    size = lax.axis_size(axis)
    pairs = [(i, i + by) for i in range(size) if 0 <= i + by < size]
    return lax.ppermute(x, axis, pairs)


def flipped(x, axis, by):
    return lax.ppermute(x, axis, [(i, i ^ by) for i in range(lax.axis_size(axis))])


def routed_shards(
    queries, keys, values, doc_ids, norm_gain, expert_ids, route_weights, w_in, w_out
):
    block_len, heads_dev, head_dim = queries.shape
    seq_count = lax.axis_size("seq")
    exp_count = lax.axis_size("exp")
    seq_index = lax.axis_index("seq")
    reach_blocks = min(-(-WINDOW // block_len), seq_count - 1)
    own_keys = keys[:, 0, :]
    own_values = values[:, 0, :]
    key_list = [own_keys]
    value_list = [own_values]
    for distance in range(1, reach_blocks + 1):
        far_keys, far_values = shifted((own_keys, own_values), "seq", distance)
        key_list.insert(0, far_keys)
        value_list.insert(0, far_values)
    near_keys = jnp.concatenate(key_list, axis=0)
    near_values = jnp.concatenate(value_list, axis=0)
    key_count = near_keys.shape[0]
    query_rows = jnp.transpose(queries, (1, 0, 2)).reshape(heads_dev * block_len, head_dim)
    score = lax.dot_general(
        query_rows, near_keys, (((1,), (1,)), ((), ())), preferred_element_type=jnp.float32
    )
    score = score * (1.0 / head_dim**0.5)
    query_pos = seq_index * block_len + jnp.arange(block_len, dtype=jnp.int32)
    key_pos = (seq_index - reach_blocks) * block_len + jnp.arange(key_count, dtype=jnp.int32)
    padded_docs = jnp.concatenate(
        [jnp.full((reach_blocks * block_len,), -1, jnp.int32), doc_ids], axis=0
    )
    key_docs = lax.dynamic_slice_in_dim(padded_docs, seq_index * block_len, key_count, 0)
    query_docs = lax.dynamic_slice_in_dim(doc_ids, seq_index * block_len, block_len, 0)
    allowed = (key_pos[None, :] <= query_pos[:, None]) & (
        query_pos[:, None] - key_pos[None, :] < WINDOW
    )
    allowed = allowed & (key_pos[None, :] >= 0) & (query_docs[:, None] == key_docs[None, :])
    allowed = jnp.tile(allowed, (heads_dev, 1))
    score = jnp.where(allowed, score, -jnp.inf)
    top_score = jnp.max(score, axis=1, keepdims=True)
    weights = jnp.where(allowed, jnp.exp(score - top_score), 0.0)
    probs = (weights / jnp.sum(weights, axis=1, keepdims=True)).astype(jnp.bfloat16)
    attended = jnp.dot(probs, near_values, preferred_element_type=jnp.float32).astype(jnp.bfloat16)
    attended = jnp.transpose(attended.reshape(heads_dev, block_len, head_dim), (1, 0, 2)).reshape(
        block_len, heads_dev * head_dim
    )
    attn = lax.all_to_all(attended, "exp", split_axis=0, concat_axis=1, tiled=True)
    token_count = attn.shape[0]
    width = attn.shape[1]
    attn_float = attn.astype(jnp.float32)
    mean_square = jnp.mean(attn_float * attn_float, axis=1, keepdims=True)
    normed = (attn_float * lax.rsqrt(mean_square + epsilon) * norm_gain[None, :]).astype(
        jnp.bfloat16
    )
    capacity = max((token_count + 2) // 3, 2 * token_count // exp_count)
    flat_ids = expert_ids.reshape(token_count * 2)
    onehot = (flat_ids[:, None] == jnp.arange(exp_count, dtype=jnp.int32)[None, :]).astype(
        jnp.int32
    )
    earlier = jnp.cumsum(onehot, axis=0) - onehot
    slot = jnp.sum(earlier * onehot, axis=1)
    local_code = (flat_ids * capacity + slot).reshape(token_count, 2)
    slot_range = jnp.arange(exp_count * capacity, dtype=jnp.int32)
    first_hit = local_code[:, 0:1] == slot_range[None, :]
    second_hit = local_code[:, 1:2] == slot_range[None, :]
    placing = jnp.transpose((first_hit | second_hit).astype(jnp.bfloat16))
    outgoing = jnp.dot(placing, normed, preferred_element_type=jnp.float32).astype(jnp.bfloat16)
    arrived = lax.all_to_all(
        outgoing.reshape(exp_count, capacity, width), "exp", split_axis=0, concat_axis=0, tiled=True
    )
    row_count = exp_count * capacity
    arrived = arrived.reshape(row_count, width)
    weight_in = w_in[0]
    weight_out = w_out[0]
    hidden = jax.nn.silu(
        jnp.dot(
            lax.all_gather(arrived, "seq", axis=0, tiled=True),
            weight_in,
            preferred_element_type=jnp.float32,
        )
    ).astype(jnp.bfloat16)
    summed = lax.psum_scatter(
        jnp.dot(hidden, weight_out, preferred_element_type=jnp.float32).astype(jnp.bfloat16),
        "seq",
        scatter_dimension=0,
        tiled=True,
    )
    expert_out = summed.reshape(exp_count, capacity, width)
    returned = lax.all_to_all(expert_out, "exp", split_axis=0, concat_axis=0, tiled=True).reshape(
        row_count, width
    )
    combine = route_weights[:, 0:1] * first_hit.astype(jnp.float32) + route_weights[
        :, 1:2
    ] * second_hit.astype(jnp.float32)
    moe_part = jnp.dot(
        combine,
        returned.astype(jnp.float32),
        precision=lax.Precision.HIGHEST,
        preferred_element_type=jnp.float32,
    )
    return (attn_float + moe_part).astype(jnp.bfloat16)


def attend_kernel(block_len, scale, *refs):
    place_ref, query_ref, doc_row, *packs = refs[:-4]
    out_ref, marked_ref, keys_ref, values_ref = refs[-4:]
    place = place_ref[0]
    lanes = packs[0].shape[1]
    for i, pack in enumerate(packs):
        rows = pl.ds(pl.multiple_of((place ^ i) * block_len, block_len), block_len)
        keys_ref[rows] = pack[0:block_len]
        values_ref[rows] = pack[block_len : 2 * block_len]
        marked_ref[block_len:, i * lanes : (i + 1) * lanes] = pack[2 * block_len :]
    marked_ref[block_len:, len(packs) * lanes :] = jnp.zeros(
        (marked_ref.shape[0] - block_len, marked_ref.shape[1] - len(packs) * lanes), jnp.bfloat16
    )
    start = pl.multiple_of(place * block_len, block_len)
    query_pos = start + lax.broadcasted_iota(jnp.int32, (block_len, 1), 0)
    key_pos = lax.broadcasted_iota(jnp.int32, doc_row.shape, 1)
    key_doc = doc_row[...]
    query_doc = jnp.sum(jnp.where(query_pos == key_pos, key_doc, 0), axis=1, keepdims=True)
    allowed = (key_pos <= query_pos) & (query_pos - key_pos < WINDOW) & (query_doc == key_doc)
    head_dim = query_ref.shape[2]
    heads = range(query_ref.shape[0])
    scores = [
        lax.dot_general(
            query_ref[head],
            keys_ref[...],
            (((1,), (1,)), ((), ())),
            preferred_element_type=jnp.float32,
        )
        for head in heads
    ]
    scores = [jnp.where(allowed, score * scale, -jnp.inf) for score in scores]
    tops = [jnp.max(score, axis=1, keepdims=True) for score in scores]
    weights = [jnp.exp(score - top) for score, top in zip(scores, tops)]
    inverses = [1.0 / jnp.sum(weight, axis=1, keepdims=True) for weight in weights]
    for head in heads:
        columns = slice(head * head_dim, (head + 1) * head_dim)
        attended = jnp.dot(
            (weights[head] * inverses[head]).astype(jnp.bfloat16),
            values_ref[...],
            preferred_element_type=jnp.float32,
        ).astype(jnp.bfloat16)
        out_ref[:, columns] = attended
        marked_ref[0:block_len, columns] = attended


def experts_kernel(seq_count, group, order, *refs):
    exp_count = len(order)
    place_ref, gain_hbm, w_in_hbm, w_out_hbm = refs[:4]
    marked = refs[4 : 4 + exp_count]
    refs = refs[4 + exp_count :]
    blocks = {0: marked}
    for d in group:
        if d:
            blocks[d], refs = refs[:exp_count], refs[exp_count:]
    kept, sent, refs = refs[: len(group)], refs[len(group) : 2 * len(group)], refs[2 * len(group) :]
    if 0 in group:
        own_ref, *refs, split_ref = refs
    hidden_ref, share_ref, gain_ref, w_in_ref, w_out_ref, sems = refs
    place = place_ref[0]
    block_len, token_count = marked[0].shape[0] - 16, hidden_ref.shape[1]
    part_width = marked[0].shape[1]
    width = part_width * exp_count
    lanes = 128

    def rows_of(j):
        return pl.ds(pl.multiple_of((place ^ j) * part_width, part_width), part_width)

    reads = [
        pltpu.make_async_copy(w_in_hbm.at[0, rows_of(j)], w_in_ref.at[j], sems.at[j])
        for j in range(exp_count)
    ]
    reads.append(pltpu.make_async_copy(w_out_hbm.at[0], w_out_ref, sems.at[exp_count]))
    reads.insert(0, pltpu.make_async_copy(gain_hbm, gain_ref, sems.at[exp_count + 1]))
    for read in reads:
        read.start()

    share_ref[...] = jnp.zeros_like(share_ref)
    for j in range(exp_count):
        share = marked[j][block_len:].astype(jnp.float32)
        row = lax.broadcasted_iota(jnp.int32, share.shape, 0)
        share = jnp.where(row % exp_count == place, share, 0.0)
        share = jnp.sum(share, axis=0, keepdims=True)
        for i, d in enumerate(group):
            line = i * exp_count + order.index(j)
            share_ref[line : line + 1] = share[:, d * lanes : (d + 1) * lanes]
    share = share_ref[...].T
    weight = jnp.concatenate(
        [share[:token_count, i : i + 1] for i in range(len(group) * exp_count)], axis=0
    )

    reads[0].wait()
    squares = [jnp.zeros((block_len, lanes), jnp.float32)] * len(group)
    hidden = None
    for j in range(exp_count):
        source = place ^ j
        gain = gain_ref[source]
        gained = []
        for i, d in enumerate(group):
            value = blocks[d][j][0:block_len].astype(jnp.float32)
            square = value * value
            for start in range(0, part_width, lanes):
                squares[i] = squares[i] + square[:, start : start + lanes]
            gained.append((value * gain).astype(jnp.bfloat16))
            if d == 0:
                split_ref[...] = value.reshape(exp_count, token_count, part_width)
                own_ref[source] = split_ref[place].astype(jnp.bfloat16)
        reads[1 + j].wait()
        product = jnp.dot(
            jnp.concatenate(gained, axis=0), w_in_ref[j], preferred_element_type=jnp.float32
        )
        hidden = product if hidden is None else hidden + product
    mean_square = jnp.sum(jnp.concatenate(squares, axis=0), axis=1, keepdims=True) * (1.0 / width)
    hidden = hidden * lax.rsqrt(mean_square + epsilon)
    hidden = hidden * (1.0 / (1.0 + jnp.exp(-hidden)))
    hidden_ref[...] = hidden.reshape(len(group) * exp_count, token_count, hidden.shape[1])
    hidden = jnp.concatenate(
        [hidden_ref[i * exp_count + (place ^ j)] for i in range(len(group)) for j in order], axis=0
    ).astype(jnp.bfloat16)
    half = block_len // 2
    reads[1 + exp_count].wait()
    for start in range(0, width, part_width):
        columns = slice(start, start + part_width)
        product = jnp.dot(hidden, w_out_ref[:, columns], preferred_element_type=jnp.float32)
        product = (product * weight).astype(jnp.bfloat16)
        for i in range(len(group)):
            low = i * block_len
            kept[i][:, columns] = product[low : low + half]
            sent[i][:, columns] = product[low + half : low + block_len]


def vmem():
    return pl.BlockSpec(memory_space=pltpu.VMEM)


def anywhere():
    return pl.BlockSpec(memory_space=pltpu.HBM)


def gathered_shards(
    queries, keys, values, doc_ids, norm_gain, expert_ids, route_weights, w_in, w_out
):
    block_len, heads_dev, head_dim = queries.shape
    seq_count = lax.axis_size("seq")
    exp_count = lax.axis_size("exp")
    seq_index = lax.axis_index("seq")
    exp_index = lax.axis_index("exp")
    token_count = expert_ids.shape[0]
    part_width = heads_dev * head_dim
    width = part_width * exp_count
    hidden_width = w_in.shape[2]
    half = block_len // 2
    far = range(1, seq_count)

    named = expert_ids[:, :, None] == jnp.arange(exp_count, dtype=jnp.int32)[None, None, :]
    rest = jnp.sum(jnp.where(named, route_weights[:, :, None], 0.0), axis=1).T
    pieces = []
    for _ in range(3):
        piece = lax.reduce_precision(rest, 8, 7)
        pieces.append(piece.astype(jnp.bfloat16))
        rest = rest - piece
    pieces = jnp.concatenate(pieces, axis=0)
    pieces = jnp.pad(pieces, ((0, 16 - 3 * exp_count), (0, head_dim - token_count)))
    pack = jnp.concatenate([keys[:, 0, :], values[:, 0, :], pieces], axis=0)
    packs = [pack] + [flipped(pack, "seq", d) for d in far]

    heads, pack = lax.optimization_barrier((jnp.transpose(queries, (1, 0, 2)), pack))
    heads = heads * jnp.bfloat16(0.125)
    packs[0] = pack

    attended, marked = pl.pallas_call(
        functools.partial(attend_kernel, block_len, 8.0 / head_dim**0.5),
        out_shape=[
            jax.ShapeDtypeStruct((block_len, part_width), jnp.bfloat16),
            jax.ShapeDtypeStruct((block_len + 16, part_width), jnp.bfloat16),
        ],
        in_specs=[pl.BlockSpec(memory_space=pltpu.SMEM)] + [vmem()] * (seq_count + 2),
        out_specs=[vmem()] * 2,
        scratch_shapes=[pltpu.VMEM((seq_count * block_len, head_dim), jnp.bfloat16)] * 2,
        compiler_params=pltpu.CompilerParams(vmem_limit_bytes=8 << 20),
        cost_estimate=pl.CostEstimate(
            flops=4 * heads_dev * block_len * seq_count * block_len * head_dim,
            bytes_accessed=1 << 20,
            transcendentals=heads_dev * block_len * seq_count * block_len,
        ),
        name="attend",
    )(seq_index.reshape(1), heads, doc_ids.reshape(1, -1), *packs)

    first = [seq_count - 1, 1]
    second = [d for d in range(seq_count - 2, -1, -1) if d not in first]
    blocks = {(d, 0): flipped(attended, "seq", d) for d in first}
    blocks[0, 0] = marked
    blocks |= {(d, 0): flipped(attended, "seq", d) for d in second if d}
    bit = exp_count // 2
    while bit:
        blocks |= {(d, j ^ bit): flipped(block, "exp", bit) for (d, j), block in blocks.items()}
        bit //= 2

    order = [j for j in range(exp_count) if not j & 1] + [j for j in range(exp_count) if j & 1]
    gain = norm_gain.reshape(exp_count, 1, part_width)
    weights = [pltpu.with_memory_space_constraint(w, pltpu.HBM) for w in (gain, w_in, w_out)]

    def experts(group):
        size = len(group)
        operands = [blocks[0, j] for j in range(exp_count)]
        operands += [blocks[d, j] for d in group if d for j in range(exp_count)]
        out_shape = [jax.ShapeDtypeStruct((half, width), jnp.bfloat16)] * (2 * size)
        scratch = [
            pltpu.VMEM((size * exp_count, token_count, hidden_width), jnp.float32),
            pltpu.VMEM((head_dim, head_dim), jnp.float32),
            pltpu.VMEM((exp_count, 1, part_width), jnp.float32),
            pltpu.VMEM((exp_count, part_width, hidden_width), jnp.bfloat16),
            pltpu.VMEM((hidden_width, width), jnp.bfloat16),
            pltpu.SemaphoreType.DMA((exp_count + 2,)),
        ]
        if 0 in group:
            split = (exp_count, token_count, part_width)
            out_shape.append(jax.ShapeDtypeStruct(split, jnp.bfloat16))
            scratch.append(pltpu.VMEM(split, jnp.float32))
        in_specs = [pl.BlockSpec(memory_space=pltpu.SMEM)] + [vmem()] * (3 + len(operands))
        in_specs[1:4] = [anywhere()] * 3
        outs = pl.pallas_call(
            functools.partial(experts_kernel, seq_count, group, order),
            out_shape=out_shape,
            in_specs=in_specs,
            out_specs=[vmem()] * len(out_shape),
            scratch_shapes=scratch,
            compiler_params=pltpu.CompilerParams(vmem_limit_bytes=16 << 20),
            cost_estimate=pl.CostEstimate(
                flops=4 * size * block_len * width * hidden_width,
                bytes_accessed=8 << 20,
                transcendentals=size * block_len * hidden_width,
            ),
            name="experts",
        )(exp_index.reshape(1), *weights, *operands)
        return dict(zip(group, zip(outs[:size], outs[size : 2 * size]))), outs[-1]

    def send(returned):
        sums = {}
        for d, (kept, sent) in returned.items():
            both = kept.astype(jnp.float32) + flipped(sent, "exp", 1).astype(jnp.float32)
            sums[d] = both[:token_count], both[token_count:].astype(jnp.bfloat16)
        return sums

    early, _ = experts(first)
    early = send(early)
    late, own = experts(second)
    late = send(late)
    total = jnp.transpose(own, (1, 0, 2)).reshape(token_count, width).astype(jnp.float32)
    for d, (mine, away) in sorted((early | late).items(), reverse=True):
        mine = mine + flipped(away, "exp", 2).astype(jnp.float32)
        if d:
            mine = flipped(mine.astype(jnp.bfloat16), "seq", d).astype(jnp.float32)
        total = total + mine
    return total.astype(jnp.bfloat16)


def solution(mesh):
    placed = (
        P(("dp", "seq"), "exp", None),
        P(("dp", "seq"), "exp", None),
        P(("dp", "seq"), "exp", None),
        P("dp"),
        P(),
        P(("dp", "seq", "exp"), None),
        P(("dp", "seq", "exp"), None),
        P("exp", None, "seq"),
        P("exp", "seq", None),
    )
    small = mesh.shape["seq"] == 4 and mesh.shape["exp"] == 4
    return jax.shard_map(
        gathered_shards if small else routed_shards,
        mesh=mesh,
        in_specs=placed,
        out_specs=P(("dp", "seq", "exp"), None),
        check_vma=False,
    )
```

```python
import functools

import jax
import jax.numpy as jnp
from jax import lax
from jax.experimental import pallas as pl
from jax.experimental.pallas import tpu as pltpu
from jax.sharding import PartitionSpec as P

WINDOW = 2048


epsilon = 1e-05


def shifted(x, axis, by):
    size = lax.axis_size(axis)
    pairs = [(i, i + by) for i in range(size) if 0 <= i + by < size]
    return lax.ppermute(x, axis, pairs)


def flipped(x, axis, by):
    return lax.ppermute(x, axis, [(i, i ^ by) for i in range(lax.axis_size(axis))])


def routed_shards(
    queries, keys, values, doc_ids, norm_gain, expert_ids, route_weights, w_in, w_out
):
    block_len, heads_dev, head_dim = queries.shape
    seq_count = lax.axis_size("seq")
    exp_count = lax.axis_size("exp")
    seq_index = lax.axis_index("seq")
    reach_blocks = min(-(-WINDOW // block_len), seq_count - 1)
    own_keys = keys[:, 0, :]
    own_values = values[:, 0, :]
    key_list = [own_keys]
    value_list = [own_values]
    for distance in range(1, reach_blocks + 1):
        far_keys, far_values = shifted((own_keys, own_values), "seq", distance)
        key_list.insert(0, far_keys)
        value_list.insert(0, far_values)
    near_keys = jnp.concatenate(key_list, axis=0)
    near_values = jnp.concatenate(value_list, axis=0)
    key_count = near_keys.shape[0]
    query_rows = jnp.transpose(queries, (1, 0, 2)).reshape(heads_dev * block_len, head_dim)
    score = lax.dot_general(
        query_rows, near_keys, (((1,), (1,)), ((), ())), preferred_element_type=jnp.float32
    )
    score = score * (1.0 / head_dim**0.5)
    query_pos = seq_index * block_len + jnp.arange(block_len, dtype=jnp.int32)
    key_pos = (seq_index - reach_blocks) * block_len + jnp.arange(key_count, dtype=jnp.int32)
    padded_docs = jnp.concatenate(
        [jnp.full((reach_blocks * block_len,), -1, jnp.int32), doc_ids], axis=0
    )
    key_docs = lax.dynamic_slice_in_dim(padded_docs, seq_index * block_len, key_count, 0)
    query_docs = lax.dynamic_slice_in_dim(doc_ids, seq_index * block_len, block_len, 0)
    allowed = (key_pos[None, :] <= query_pos[:, None]) & (
        query_pos[:, None] - key_pos[None, :] < WINDOW
    )
    allowed = allowed & (key_pos[None, :] >= 0) & (query_docs[:, None] == key_docs[None, :])
    allowed = jnp.tile(allowed, (heads_dev, 1))
    score = jnp.where(allowed, score, -jnp.inf)
    top_score = jnp.max(score, axis=1, keepdims=True)
    weights = jnp.where(allowed, jnp.exp(score - top_score), 0.0)
    probs = (weights / jnp.sum(weights, axis=1, keepdims=True)).astype(jnp.bfloat16)
    attended = jnp.dot(probs, near_values, preferred_element_type=jnp.float32).astype(jnp.bfloat16)
    attended = jnp.transpose(attended.reshape(heads_dev, block_len, head_dim), (1, 0, 2)).reshape(
        block_len, heads_dev * head_dim
    )
    attn = lax.all_to_all(attended, "exp", split_axis=0, concat_axis=1, tiled=True)
    token_count = attn.shape[0]
    width = attn.shape[1]
    attn_float = attn.astype(jnp.float32)
    mean_square = jnp.mean(attn_float * attn_float, axis=1, keepdims=True)
    normed = (attn_float * lax.rsqrt(mean_square + epsilon) * norm_gain[None, :]).astype(
        jnp.bfloat16
    )
    capacity = max((token_count + 2) // 3, 2 * token_count // exp_count)
    flat_ids = expert_ids.reshape(token_count * 2)
    onehot = (flat_ids[:, None] == jnp.arange(exp_count, dtype=jnp.int32)[None, :]).astype(
        jnp.int32
    )
    earlier = jnp.cumsum(onehot, axis=0) - onehot
    slot = jnp.sum(earlier * onehot, axis=1)
    local_code = (flat_ids * capacity + slot).reshape(token_count, 2)
    slot_range = jnp.arange(exp_count * capacity, dtype=jnp.int32)
    first_hit = local_code[:, 0:1] == slot_range[None, :]
    second_hit = local_code[:, 1:2] == slot_range[None, :]
    placing = jnp.transpose((first_hit | second_hit).astype(jnp.bfloat16))
    outgoing = jnp.dot(placing, normed, preferred_element_type=jnp.float32).astype(jnp.bfloat16)
    arrived = lax.all_to_all(
        outgoing.reshape(exp_count, capacity, width), "exp", split_axis=0, concat_axis=0, tiled=True
    )
    row_count = exp_count * capacity
    arrived = arrived.reshape(row_count, width)
    weight_in = w_in[0]
    weight_out = w_out[0]
    hidden = jax.nn.silu(
        jnp.dot(
            lax.all_gather(arrived, "seq", axis=0, tiled=True),
            weight_in,
            preferred_element_type=jnp.float32,
        )
    ).astype(jnp.bfloat16)
    summed = lax.psum_scatter(
        jnp.dot(hidden, weight_out, preferred_element_type=jnp.float32).astype(jnp.bfloat16),
        "seq",
        scatter_dimension=0,
        tiled=True,
    )
    expert_out = summed.reshape(exp_count, capacity, width)
    returned = lax.all_to_all(expert_out, "exp", split_axis=0, concat_axis=0, tiled=True).reshape(
        row_count, width
    )
    combine = route_weights[:, 0:1] * first_hit.astype(jnp.float32) + route_weights[
        :, 1:2
    ] * second_hit.astype(jnp.float32)
    moe_part = jnp.dot(
        combine,
        returned.astype(jnp.float32),
        precision=lax.Precision.HIGHEST,
        preferred_element_type=jnp.float32,
    )
    return (attn_float + moe_part).astype(jnp.bfloat16)


def attend_kernel(block_len, scale, *refs):
    place_ref, query_ref, doc_row, *packs = refs[:-4]
    out_ref, marked_ref, keys_ref, values_ref = refs[-4:]
    place = place_ref[0]
    lanes = packs[0].shape[1]
    for i, pack in enumerate(packs):
        rows = pl.ds(pl.multiple_of((place ^ i) * block_len, block_len), block_len)
        keys_ref[rows] = pack[0:block_len]
        values_ref[rows] = pack[block_len : 2 * block_len]
        marked_ref[block_len:, i * lanes : (i + 1) * lanes] = pack[2 * block_len :]
    marked_ref[block_len:, len(packs) * lanes :] = jnp.zeros(
        (marked_ref.shape[0] - block_len, marked_ref.shape[1] - len(packs) * lanes), jnp.bfloat16
    )
    start = pl.multiple_of(place * block_len, block_len)
    query_pos = start + lax.broadcasted_iota(jnp.int32, (block_len, 1), 0)
    key_pos = lax.broadcasted_iota(jnp.int32, doc_row.shape, 1)
    key_doc = doc_row[...]
    query_doc = jnp.sum(jnp.where(query_pos == key_pos, key_doc, 0), axis=1, keepdims=True)
    allowed = (key_pos <= query_pos) & (query_pos - key_pos < WINDOW) & (query_doc == key_doc)
    head_dim = query_ref.shape[2]
    heads = range(query_ref.shape[0])
    scores = [
        lax.dot_general(
            query_ref[head],
            keys_ref[...],
            (((1,), (1,)), ((), ())),
            preferred_element_type=jnp.float32,
        )
        for head in heads
    ]
    scores = [jnp.where(allowed, score * scale, -jnp.inf) for score in scores]
    tops = [jnp.max(score, axis=1, keepdims=True) for score in scores]
    weights = [jnp.exp(score - top) for score, top in zip(scores, tops)]
    inverses = [1.0 / jnp.sum(weight, axis=1, keepdims=True) for weight in weights]
    for head in heads:
        columns = slice(head * head_dim, (head + 1) * head_dim)
        attended = jnp.dot(
            (weights[head] * inverses[head]).astype(jnp.bfloat16),
            values_ref[...],
            preferred_element_type=jnp.float32,
        ).astype(jnp.bfloat16)
        out_ref[:, columns] = attended
        marked_ref[0:block_len, columns] = attended


def experts_kernel(seq_count, group, order, *refs):
    exp_count = len(order)
    place_ref, gain_hbm, w_in_hbm, w_out_hbm = refs[:4]
    marked = refs[4 : 4 + exp_count]
    refs = refs[4 + exp_count :]
    blocks = {0: marked}
    for d in group:
        if d:
            blocks[d], refs = refs[:exp_count], refs[exp_count:]
    kept, sent, refs = refs[: len(group)], refs[len(group) : 2 * len(group)], refs[2 * len(group) :]
    if 0 in group:
        own_ref, *refs, split_ref = refs
    hidden_ref, share_ref, gain_ref, w_in_ref, w_out_ref, sum_ref, sems = refs
    place = place_ref[0]
    block_len, token_count = marked[0].shape[0] - 16, hidden_ref.shape[1]
    part_width = marked[0].shape[1]
    width = part_width * exp_count
    lanes = 128

    def rows_of(j):
        return pl.ds(pl.multiple_of((place ^ j) * part_width, part_width), part_width)

    reads = [
        pltpu.make_async_copy(w_in_hbm.at[0, rows_of(j)], w_in_ref.at[j], sems.at[j])
        for j in range(exp_count)
    ]
    depth = hidden_ref.shape[2] // 2
    reads += [
        pltpu.make_async_copy(
            w_out_hbm.at[0, i * depth : (i + 1) * depth],
            w_out_ref.at[i * depth : (i + 1) * depth],
            sems.at[exp_count + i],
        )
        for i in range(2)
    ]
    reads.insert(0, pltpu.make_async_copy(gain_hbm, gain_ref, sems.at[exp_count + 2]))
    for read in reads:
        read.start()

    share_ref[...] = jnp.zeros_like(share_ref)
    for j in range(exp_count):
        share = marked[j][block_len:].astype(jnp.float32)
        row = lax.broadcasted_iota(jnp.int32, share.shape, 0)
        share = jnp.where(row % exp_count == place, share, 0.0)
        share = jnp.sum(share, axis=0, keepdims=True)
        for i, d in enumerate(group):
            line = i * exp_count + order.index(j)
            share_ref[line : line + 1] = share[:, d * lanes : (d + 1) * lanes]
    share = share_ref[...].T
    weight = jnp.concatenate(
        [share[:token_count, i : i + 1] for i in range(len(group) * exp_count)], axis=0
    )

    reads[0].wait()
    squares = [jnp.zeros((block_len, lanes), jnp.float32)] * len(group)
    hidden = None
    for j in range(exp_count):
        source = place ^ j
        gain = gain_ref[source]
        gained = []
        for i, d in enumerate(group):
            value = blocks[d][j][0:block_len].astype(jnp.float32)
            square = value * value
            for start in range(0, part_width, lanes):
                squares[i] = squares[i] + square[:, start : start + lanes]
            gained.append((value * gain).astype(jnp.bfloat16))
            if d == 0:
                split_ref[...] = value.reshape(exp_count, token_count, part_width)
                own_ref[source] = split_ref[place].astype(jnp.bfloat16)
        reads[1 + j].wait()
        product = jnp.dot(
            jnp.concatenate(gained, axis=0), w_in_ref[j], preferred_element_type=jnp.float32
        )
        hidden = product if hidden is None else hidden + product
    mean_square = jnp.sum(jnp.concatenate(squares, axis=0), axis=1, keepdims=True) * (1.0 / width)
    hidden = hidden * lax.rsqrt(mean_square + epsilon)
    hidden = hidden * (1.0 / (1.0 + jnp.exp(-hidden)))
    hidden_ref[...] = hidden.reshape(len(group) * exp_count, token_count, hidden.shape[1])
    hidden = jnp.concatenate(
        [hidden_ref[i * exp_count + (place ^ j)] for i in range(len(group)) for j in order], axis=0
    ).astype(jnp.bfloat16)
    half = block_len // 2
    tiles = [slice(start, start + part_width) for start in range(0, width, part_width)]
    reads[1 + exp_count].wait()
    for columns in tiles:
        sum_ref[:, columns] = jnp.dot(
            hidden[:, :depth], w_out_ref[:depth, columns], preferred_element_type=jnp.float32
        )
    reads[2 + exp_count].wait()
    for columns in tiles:
        product = sum_ref[:, columns] + jnp.dot(
            hidden[:, depth:], w_out_ref[depth:, columns], preferred_element_type=jnp.float32
        )
        product = (product * weight).astype(jnp.bfloat16)
        for i in range(len(group)):
            low = i * block_len
            kept[i][:, columns] = product[low : low + half]
            sent[i][:, columns] = product[low + half : low + block_len]


def after(value, *others):
    return lax.optimization_barrier((value, *others))[0]


def vmem():
    return pl.BlockSpec(memory_space=pltpu.VMEM)


def anywhere():
    return pl.BlockSpec(memory_space=pltpu.HBM)


def gathered_shards(
    queries, keys, values, doc_ids, norm_gain, expert_ids, route_weights, w_in, w_out
):
    block_len, heads_dev, head_dim = queries.shape
    seq_count = lax.axis_size("seq")
    exp_count = lax.axis_size("exp")
    seq_index = lax.axis_index("seq")
    exp_index = lax.axis_index("exp")
    token_count = expert_ids.shape[0]
    part_width = heads_dev * head_dim
    width = part_width * exp_count
    hidden_width = w_in.shape[2]
    half = block_len // 2
    far = range(1, seq_count)

    named = expert_ids[:, :, None] == jnp.arange(exp_count, dtype=jnp.int32)[None, None, :]
    rest = jnp.sum(jnp.where(named, route_weights[:, :, None], 0.0), axis=1).T
    pieces = []
    for _ in range(3):
        piece = lax.reduce_precision(rest, 8, 7)
        pieces.append(piece.astype(jnp.bfloat16))
        rest = rest - piece
    pieces = jnp.concatenate(pieces, axis=0)
    pieces = jnp.pad(pieces, ((0, 16 - 3 * exp_count), (0, head_dim - token_count)))
    pack = jnp.concatenate([keys[:, 0, :], values[:, 0, :], pieces], axis=0)
    packs = [pack] + [flipped(pack, "seq", d) for d in far]

    heads, pack = lax.optimization_barrier((jnp.transpose(queries, (1, 0, 2)), pack))
    heads = heads * jnp.bfloat16(0.125)
    packs[0] = pack

    attended, marked = pl.pallas_call(
        functools.partial(attend_kernel, block_len, 8.0 / head_dim**0.5),
        out_shape=[
            jax.ShapeDtypeStruct((block_len, part_width), jnp.bfloat16),
            jax.ShapeDtypeStruct((block_len + 16, part_width), jnp.bfloat16),
        ],
        in_specs=[pl.BlockSpec(memory_space=pltpu.SMEM)] + [vmem()] * (seq_count + 2),
        out_specs=[vmem()] * 2,
        scratch_shapes=[pltpu.VMEM((seq_count * block_len, head_dim), jnp.bfloat16)] * 2,
        compiler_params=pltpu.CompilerParams(vmem_limit_bytes=8 << 20),
        cost_estimate=pl.CostEstimate(
            flops=4 * heads_dev * block_len * seq_count * block_len * head_dim,
            bytes_accessed=1 << 20,
            transcendentals=heads_dev * block_len * seq_count * block_len,
        ),
        name="attend",
    )(seq_index.reshape(1), heads, doc_ids.reshape(1, -1), *packs)

    first, second = [3, 1], [2, 0]
    far_bit = exp_count // 2
    blocks = {(d, 0): flipped(attended, "seq", d) for d in [3, 1, 2]}
    blocks[0, 0] = marked

    def spread(d, bit):
        for j in range(0, exp_count, 2 * bit):
            blocks[d, j ^ bit] = flipped(blocks[d, j], "exp", bit)

    for d in [0, 3, 1, 2]:
        spread(d, 2)
        blocks[d, 1], blocks[d, 3] = flipped(blocks[d, 0], "exp", 1), flipped(blocks[d, 2], "exp", 1)
    blocks[3, 2] = after(blocks[3, 2], blocks[2, 0])
    blocks[3, 3] = flipped(blocks[3, 2], 'exp', 1)
    order = [j for j in range(exp_count) if not j & 1] + [j for j in range(exp_count) if j & 1]
    gain = norm_gain.reshape(exp_count, 1, part_width)
    weights = [pltpu.with_memory_space_constraint(w, pltpu.HBM) for w in (gain, w_in, w_out)]

    def experts(group):
        size = len(group)
        operands = [blocks[0, j] for j in range(exp_count)]
        operands += [blocks[d, j] for d in group if d for j in range(exp_count)]
        out_shape = [jax.ShapeDtypeStruct((half, width), jnp.bfloat16)] * (2 * size)
        scratch = [
            pltpu.VMEM((size * exp_count, token_count, hidden_width), jnp.float32),
            pltpu.VMEM((head_dim, head_dim), jnp.float32),
            pltpu.VMEM((exp_count, 1, part_width), jnp.float32),
            pltpu.VMEM((exp_count, part_width, hidden_width), jnp.bfloat16),
            pltpu.VMEM((hidden_width, width), jnp.bfloat16),
            pltpu.VMEM((size * block_len, width), jnp.float32),
            pltpu.SemaphoreType.DMA((exp_count + 3,)),
        ]
        if 0 in group:
            split = (exp_count, token_count, part_width)
            out_shape.append(jax.ShapeDtypeStruct(split, jnp.bfloat16))
            scratch.append(pltpu.VMEM(split, jnp.float32))
        in_specs = [pl.BlockSpec(memory_space=pltpu.SMEM)] + [vmem()] * (3 + len(operands))
        in_specs[1:4] = [anywhere()] * 3
        outs = pl.pallas_call(
            functools.partial(experts_kernel, seq_count, group, order),
            out_shape=out_shape,
            in_specs=in_specs,
            out_specs=[vmem()] * len(out_shape),
            scratch_shapes=scratch,
            compiler_params=pltpu.CompilerParams(vmem_limit_bytes=16 << 20),
            cost_estimate=pl.CostEstimate(
                flops=4 * size * block_len * width * hidden_width,
                bytes_accessed=8 << 20,
                transcendentals=size * block_len * hidden_width,
            ),
            name="experts",
        )(exp_index.reshape(1), *weights, *operands)
        return dict(zip(group, zip(outs[:size], outs[size : 2 * size]))), outs[-1]

    def send(returned):
        sums = {}
        for d, (kept, sent) in returned.items():
            both = kept.astype(jnp.float32) + flipped(sent, "exp", 1).astype(jnp.float32)
            sums[d] = both[:token_count], both[token_count:].astype(jnp.bfloat16)
        return sums

    early, own_e = experts(first)
    early[3], early[1] = [(kept, after(sent, blocks[2, 2])) for kept, sent in (early[3], early[1])]
    early = send(early)
    blocks[2, 3] = after(blocks[2, 3], early[3][1])
    late, own_l = experts(second)
    own = own_e if 0 in first else own_l
    late = send(late)
    total = jnp.transpose(own, (1, 0, 2)).reshape(token_count, width).astype(jnp.float32)
    for d, (mine, away) in sorted((early | late).items(), reverse=True):
        if d == 1:
            away = after(away, late[2][1])
        came = flipped(away, "exp", 2)
        if d == 3:
            came3 = came
        mine = mine + came.astype(jnp.float32)
        if d:
            mine = flipped(mine.astype(jnp.bfloat16), "seq", d).astype(jnp.float32)
        total = total + mine
    return total.astype(jnp.bfloat16)


def solution(mesh):
    placed = (
        P(("dp", "seq"), "exp", None),
        P(("dp", "seq"), "exp", None),
        P(("dp", "seq"), "exp", None),
        P("dp"),
        P(),
        P(("dp", "seq", "exp"), None),
        P(("dp", "seq", "exp"), None),
        P("exp", None, "seq"),
        P("exp", "seq", None),
    )
    small = mesh.shape["seq"] == 4 and mesh.shape["exp"] == 4
    return jax.shard_map(
        gathered_shards if small else routed_shards,
        mesh=mesh,
        in_specs=placed,
        out_specs=P(("dp", "seq", "exp"), None),
        check_vma=False,
    )
```

```python
import functools

import jax
import jax.numpy as jnp
from jax import lax
from jax.experimental import pallas as pl
from jax.experimental.pallas import tpu as pltpu
from jax.sharding import PartitionSpec as P

WINDOW = 2048


epsilon = 1e-05

GROUPS = [[3, 1], [2, 0]]
SEQUENCE = ['z3', 'z1', 'z2', 'x0', 'd0', 'e0', 'x3', 'd3', 'x1', 'd1', 'x2', 'd2', 'e3', 'e1', 'e2', 'g0', 'r3', 'r1', 'g1', 'r2', 'r0', 'y3', 'w3', 'y2', 'w2', 'y1', 'w1', 'y0']
WAITS = {'g1': ('r3',), 'r1': ('x2',), 'r3': ('x2',), 'y1': ('r2',)}


def shifted(x, axis, by):
    size = lax.axis_size(axis)
    pairs = [(i, i + by) for i in range(size) if 0 <= i + by < size]
    return lax.ppermute(x, axis, pairs)


def flipped(x, axis, by):
    return lax.ppermute(x, axis, [(i, i ^ by) for i in range(lax.axis_size(axis))])


def routed_shards(
    queries, keys, values, doc_ids, norm_gain, expert_ids, route_weights, w_in, w_out
):
    block_len, heads_dev, head_dim = queries.shape
    seq_count = lax.axis_size("seq")
    exp_count = lax.axis_size("exp")
    seq_index = lax.axis_index("seq")
    reach_blocks = min(-(-WINDOW // block_len), seq_count - 1)
    own_keys = keys[:, 0, :]
    own_values = values[:, 0, :]
    key_list = [own_keys]
    value_list = [own_values]
    for distance in range(1, reach_blocks + 1):
        far_keys, far_values = shifted((own_keys, own_values), "seq", distance)
        key_list.insert(0, far_keys)
        value_list.insert(0, far_values)
    near_keys = jnp.concatenate(key_list, axis=0)
    near_values = jnp.concatenate(value_list, axis=0)
    key_count = near_keys.shape[0]
    query_rows = jnp.transpose(queries, (1, 0, 2)).reshape(heads_dev * block_len, head_dim)
    score = lax.dot_general(
        query_rows, near_keys, (((1,), (1,)), ((), ())), preferred_element_type=jnp.float32
    )
    score = score * (1.0 / head_dim**0.5)
    query_pos = seq_index * block_len + jnp.arange(block_len, dtype=jnp.int32)
    key_pos = (seq_index - reach_blocks) * block_len + jnp.arange(key_count, dtype=jnp.int32)
    padded_docs = jnp.concatenate(
        [jnp.full((reach_blocks * block_len,), -1, jnp.int32), doc_ids], axis=0
    )
    key_docs = lax.dynamic_slice_in_dim(padded_docs, seq_index * block_len, key_count, 0)
    query_docs = lax.dynamic_slice_in_dim(doc_ids, seq_index * block_len, block_len, 0)
    allowed = (key_pos[None, :] <= query_pos[:, None]) & (
        query_pos[:, None] - key_pos[None, :] < WINDOW
    )
    allowed = allowed & (key_pos[None, :] >= 0) & (query_docs[:, None] == key_docs[None, :])
    allowed = jnp.tile(allowed, (heads_dev, 1))
    score = jnp.where(allowed, score, -jnp.inf)
    top_score = jnp.max(score, axis=1, keepdims=True)
    weights = jnp.where(allowed, jnp.exp(score - top_score), 0.0)
    probs = (weights / jnp.sum(weights, axis=1, keepdims=True)).astype(jnp.bfloat16)
    attended = jnp.dot(probs, near_values, preferred_element_type=jnp.float32).astype(jnp.bfloat16)
    attended = jnp.transpose(attended.reshape(heads_dev, block_len, head_dim), (1, 0, 2)).reshape(
        block_len, heads_dev * head_dim
    )
    attn = lax.all_to_all(attended, "exp", split_axis=0, concat_axis=1, tiled=True)
    token_count = attn.shape[0]
    width = attn.shape[1]
    attn_float = attn.astype(jnp.float32)
    mean_square = jnp.mean(attn_float * attn_float, axis=1, keepdims=True)
    normed = (attn_float * lax.rsqrt(mean_square + epsilon) * norm_gain[None, :]).astype(
        jnp.bfloat16
    )
    capacity = max((token_count + 2) // 3, 2 * token_count // exp_count)
    flat_ids = expert_ids.reshape(token_count * 2)
    onehot = (flat_ids[:, None] == jnp.arange(exp_count, dtype=jnp.int32)[None, :]).astype(
        jnp.int32
    )
    earlier = jnp.cumsum(onehot, axis=0) - onehot
    slot = jnp.sum(earlier * onehot, axis=1)
    local_code = (flat_ids * capacity + slot).reshape(token_count, 2)
    slot_range = jnp.arange(exp_count * capacity, dtype=jnp.int32)
    first_hit = local_code[:, 0:1] == slot_range[None, :]
    second_hit = local_code[:, 1:2] == slot_range[None, :]
    placing = jnp.transpose((first_hit | second_hit).astype(jnp.bfloat16))
    outgoing = jnp.dot(placing, normed, preferred_element_type=jnp.float32).astype(jnp.bfloat16)
    arrived = lax.all_to_all(
        outgoing.reshape(exp_count, capacity, width), "exp", split_axis=0, concat_axis=0, tiled=True
    )
    row_count = exp_count * capacity
    arrived = arrived.reshape(row_count, width)
    weight_in = w_in[0]
    weight_out = w_out[0]
    hidden = jax.nn.silu(
        jnp.dot(
            lax.all_gather(arrived, "seq", axis=0, tiled=True),
            weight_in,
            preferred_element_type=jnp.float32,
        )
    ).astype(jnp.bfloat16)
    summed = lax.psum_scatter(
        jnp.dot(hidden, weight_out, preferred_element_type=jnp.float32).astype(jnp.bfloat16),
        "seq",
        scatter_dimension=0,
        tiled=True,
    )
    expert_out = summed.reshape(exp_count, capacity, width)
    returned = lax.all_to_all(expert_out, "exp", split_axis=0, concat_axis=0, tiled=True).reshape(
        row_count, width
    )
    combine = route_weights[:, 0:1] * first_hit.astype(jnp.float32) + route_weights[
        :, 1:2
    ] * second_hit.astype(jnp.float32)
    moe_part = jnp.dot(
        combine,
        returned.astype(jnp.float32),
        precision=lax.Precision.HIGHEST,
        preferred_element_type=jnp.float32,
    )
    return (attn_float + moe_part).astype(jnp.bfloat16)


def pack_kernel(
    exp_count, keys_ref, values_ref, ids_hbm, route_hbm, out_ref, ids_ref, route_ref, share_ref, sems
):
    block_len = keys_ref.shape[0]
    token_count = ids_ref.shape[1]
    copies = [
        pltpu.make_async_copy(source, target, sems.at[i])
        for i, (source, target) in enumerate(
            [
                (ids_hbm, ids_ref),
                (route_hbm, route_ref),
                (keys_ref, out_ref.at[0:block_len]),
                (values_ref, out_ref.at[block_len : 2 * block_len]),
            ]
        )
    ]
    for copy in copies:
        copy.start()
    share_ref[...] = jnp.zeros_like(share_ref)
    copies[0].wait()
    copies[1].wait()
    for expert in range(exp_count):
        rest = jnp.sum(jnp.where(ids_ref[...] == expert, route_ref[...], 0.0), axis=0, keepdims=True)
        for piece in range(3):
            row = piece * exp_count + expert
            part = rest.astype(jnp.bfloat16).astype(jnp.float32)
            share_ref[row : row + 1, 0:token_count] = part
            rest = rest - part
    out_ref[2 * block_len :] = share_ref[...].astype(jnp.bfloat16)
    copies[2].wait()
    copies[3].wait()


def attend_kernel(block_len, scale, *refs):
    place_ref, query_ref, doc_row, *packs = refs[:-4]
    out_ref, marked_ref, keys_ref, values_ref = refs[-4:]
    place = place_ref[0]
    lanes = packs[0].shape[1]
    for i, pack in enumerate(packs):
        rows = pl.ds(pl.multiple_of((place ^ i) * block_len, block_len), block_len)
        keys_ref[rows] = pack[0:block_len]
        values_ref[rows] = pack[block_len : 2 * block_len]
        marked_ref[block_len:, i * lanes : (i + 1) * lanes] = pack[2 * block_len :]
    marked_ref[block_len:, len(packs) * lanes :] = jnp.zeros(
        (marked_ref.shape[0] - block_len, marked_ref.shape[1] - len(packs) * lanes), jnp.bfloat16
    )
    start = pl.multiple_of(place * block_len, block_len)
    query_pos = start + lax.broadcasted_iota(jnp.int32, (block_len, 1), 0)
    key_pos = lax.broadcasted_iota(jnp.int32, doc_row.shape, 1)
    key_doc = doc_row[...]
    query_doc = jnp.sum(jnp.where(query_pos == key_pos, key_doc, 0), axis=1, keepdims=True)
    allowed = (key_pos <= query_pos) & (query_pos - key_pos < WINDOW) & (query_doc == key_doc)
    head_dim = query_ref.shape[2]
    heads = range(query_ref.shape[0])
    scores = [
        lax.dot_general(
            query_ref[head],
            keys_ref[...],
            (((1,), (1,)), ((), ())),
            preferred_element_type=jnp.float32,
        )
        for head in heads
    ]
    scores = [jnp.where(allowed, score * scale, -jnp.inf) for score in scores]
    tops = [jnp.max(score, axis=1, keepdims=True) for score in scores]
    weights = [jnp.exp(score - top) for score, top in zip(scores, tops)]
    inverses = [1.0 / jnp.sum(weight, axis=1, keepdims=True) for weight in weights]
    for head in heads:
        columns = slice(head * head_dim, (head + 1) * head_dim)
        attended = jnp.dot(
            (weights[head] * inverses[head]).astype(jnp.bfloat16),
            values_ref[...],
            preferred_element_type=jnp.float32,
        ).astype(jnp.bfloat16)
        out_ref[:, columns] = attended
        marked_ref[0:block_len, columns] = attended


def experts_kernel(seq_count, group, order, *refs):
    exp_count = len(order)
    place_ref, gain_hbm, w_in_hbm, w_out_hbm = refs[:4]
    marked = refs[4 : 4 + exp_count]
    refs = refs[4 + exp_count :]
    blocks = {0: marked}
    for d in group:
        if d:
            blocks[d], refs = refs[:exp_count], refs[exp_count:]
    kept, sent, refs = refs[: len(group)], refs[len(group) : 2 * len(group)], refs[2 * len(group) :]
    if 0 in group:
        own_ref, *refs, split_ref = refs
    hidden_ref, share_ref, gain_ref, w_in_ref, w_out_ref, sum_ref, sems = refs
    place = place_ref[0]
    block_len, token_count = marked[0].shape[0] - 16, hidden_ref.shape[1]
    part_width = marked[0].shape[1]
    width = part_width * exp_count
    lanes = 128

    def rows_of(j):
        return pl.ds(pl.multiple_of((place ^ j) * part_width, part_width), part_width)

    reads = [
        pltpu.make_async_copy(w_in_hbm.at[0, rows_of(j)], w_in_ref.at[j], sems.at[j])
        for j in range(exp_count)
    ]
    depth = hidden_ref.shape[2] // 2
    reads += [
        pltpu.make_async_copy(
            w_out_hbm.at[0, i * depth : (i + 1) * depth],
            w_out_ref.at[i * depth : (i + 1) * depth],
            sems.at[exp_count + i],
        )
        for i in range(2)
    ]
    reads.insert(0, pltpu.make_async_copy(gain_hbm, gain_ref, sems.at[exp_count + 2]))
    for read in reads:
        read.start()

    share_ref[...] = jnp.zeros_like(share_ref)
    for j in range(exp_count):
        share = marked[j][block_len:].astype(jnp.float32)
        row = lax.broadcasted_iota(jnp.int32, share.shape, 0)
        share = jnp.where(row % exp_count == place, share, 0.0)
        share = jnp.sum(share, axis=0, keepdims=True)
        for i, d in enumerate(group):
            line = i * exp_count + order.index(j)
            share_ref[line : line + 1] = share[:, d * lanes : (d + 1) * lanes]
    share = share_ref[...].T
    weight = jnp.concatenate(
        [share[:token_count, i : i + 1] for i in range(len(group) * exp_count)], axis=0
    )

    reads[0].wait()
    squares = [jnp.zeros((block_len, lanes), jnp.float32)] * len(group)
    hidden = None
    for j in range(exp_count):
        source = place ^ j
        gain = gain_ref[source]
        gained = []
        for i, d in enumerate(group):
            value = blocks[d][j][0:block_len].astype(jnp.float32)
            square = value * value
            for start in range(0, part_width, lanes):
                squares[i] = squares[i] + square[:, start : start + lanes]
            gained.append((value * gain).astype(jnp.bfloat16))
            if d == 0:
                split_ref[...] = value.reshape(exp_count, token_count, part_width)
                own_ref[source] = split_ref[place].astype(jnp.bfloat16)
        reads[1 + j].wait()
        product = jnp.dot(
            jnp.concatenate(gained, axis=0), w_in_ref[j], preferred_element_type=jnp.float32
        )
        hidden = product if hidden is None else hidden + product
    mean_square = jnp.sum(jnp.concatenate(squares, axis=0), axis=1, keepdims=True) * (1.0 / width)
    hidden = hidden * lax.rsqrt(mean_square + epsilon)
    hidden = hidden * (1.0 / (1.0 + jnp.exp(-hidden)))
    hidden_ref[...] = hidden.reshape(len(group) * exp_count, token_count, hidden.shape[1])
    hidden = jnp.concatenate(
        [hidden_ref[i * exp_count + (place ^ j)] for i in range(len(group)) for j in order], axis=0
    ).astype(jnp.bfloat16)
    half = block_len // 2
    tiles = [slice(start, start + part_width) for start in range(0, width, part_width)]
    reads[1 + exp_count].wait()
    for columns in tiles:
        sum_ref[:, columns] = jnp.dot(
            hidden[:, :depth], w_out_ref[:depth, columns], preferred_element_type=jnp.float32
        )
    reads[2 + exp_count].wait()
    for columns in tiles:
        product = sum_ref[:, columns] + jnp.dot(
            hidden[:, depth:], w_out_ref[depth:, columns], preferred_element_type=jnp.float32
        )
        product = (product * weight).astype(jnp.bfloat16)
        for i in range(len(group)):
            low = i * block_len
            kept[i][:, columns] = product[low : low + half]
            sent[i][:, columns] = product[low + half : low + block_len]


def vmem():
    return pl.BlockSpec(memory_space=pltpu.VMEM)


def anywhere():
    return pl.BlockSpec(memory_space=pltpu.HBM)


def gathered_shards(
    queries, keys, values, doc_ids, norm_gain, expert_ids, route_weights, w_in, w_out
):
    block_len, heads_dev, head_dim = queries.shape
    seq_count = lax.axis_size("seq")
    exp_count = lax.axis_size("exp")
    seq_index = lax.axis_index("seq")
    exp_index = lax.axis_index("exp")
    token_count = expert_ids.shape[0]
    part_width = heads_dev * head_dim
    width = part_width * exp_count
    hidden_width = w_in.shape[2]
    half = block_len // 2
    far = range(1, seq_count)

    pack = pl.pallas_call(
        functools.partial(pack_kernel, exp_count),
        out_shape=jax.ShapeDtypeStruct((2 * block_len + 16, head_dim), jnp.bfloat16),
        in_specs=[anywhere()] * 4,
        out_specs=vmem(),
        scratch_shapes=[
            pltpu.VMEM(expert_ids.shape[::-1], jnp.int32),
            pltpu.VMEM(route_weights.shape[::-1], jnp.float32),
            pltpu.VMEM((16, head_dim), jnp.float32),
            pltpu.SemaphoreType.DMA((4,)),
        ],
        compiler_params=pltpu.CompilerParams(vmem_limit_bytes=4 << 20),
        name="pack",
    )(
        *[
            pltpu.with_memory_space_constraint(x, pltpu.HBM)
            for x in (keys[:, 0, :], values[:, 0, :], expert_ids.T, route_weights.T)
        ]
    )
    packs = [pack] + [flipped(pack, "seq", d) for d in far]

    heads, pack = lax.optimization_barrier((jnp.transpose(queries, (1, 0, 2)), pack))
    heads = heads * jnp.bfloat16(0.125)
    packs[0] = pack

    attended, marked = pl.pallas_call(
        functools.partial(attend_kernel, block_len, 8.0 / head_dim**0.5),
        out_shape=[
            jax.ShapeDtypeStruct((block_len, part_width), jnp.bfloat16),
            jax.ShapeDtypeStruct((block_len + 16, part_width), jnp.bfloat16),
        ],
        in_specs=[pl.BlockSpec(memory_space=pltpu.SMEM)] + [vmem()] * (seq_count + 2),
        out_specs=[vmem()] * 2,
        scratch_shapes=[pltpu.VMEM((seq_count * block_len, head_dim), jnp.bfloat16)] * 2,
        compiler_params=pltpu.CompilerParams(vmem_limit_bytes=8 << 20),
        cost_estimate=pl.CostEstimate(
            flops=4 * heads_dev * block_len * seq_count * block_len * head_dim,
            bytes_accessed=1 << 20,
            transcendentals=heads_dev * block_len * seq_count * block_len,
        ),
        name="attend",
    )(seq_index.reshape(1), heads, doc_ids.reshape(1, -1), *packs)

    order = [j for j in range(exp_count) if not j & 1] + [j for j in range(exp_count) if j & 1]
    gain = norm_gain.reshape(exp_count, 1, part_width)
    weights = [pltpu.with_memory_space_constraint(w, pltpu.HBM) for w in (gain, w_in, w_out)]

    def experts(group, last):
        size = len(group)
        operands = list(marked_blocks)
        for d in group:
            if d:
                operands += [there[kind + str(d)] for kind in "zdx"]
                operands.append(there["e" + str(d)] if d != group[0] else last)
        out_shape = [jax.ShapeDtypeStruct((half, width), jnp.bfloat16)] * (2 * size)
        scratch = [
            pltpu.VMEM((size * exp_count, token_count, hidden_width), jnp.float32),
            pltpu.VMEM((head_dim, head_dim), jnp.float32),
            pltpu.VMEM((exp_count, 1, part_width), jnp.float32),
            pltpu.VMEM((exp_count, part_width, hidden_width), jnp.bfloat16),
            pltpu.VMEM((hidden_width, width), jnp.bfloat16),
            pltpu.VMEM((size * block_len, width), jnp.float32),
            pltpu.SemaphoreType.DMA((exp_count + 3,)),
        ]
        if 0 in group:
            split = (exp_count, token_count, part_width)
            out_shape.append(jax.ShapeDtypeStruct(split, jnp.bfloat16))
            scratch.append(pltpu.VMEM(split, jnp.float32))
        in_specs = [pl.BlockSpec(memory_space=pltpu.SMEM)] + [vmem()] * (3 + len(operands))
        in_specs[1:4] = [anywhere()] * 3
        outs = pl.pallas_call(
            functools.partial(experts_kernel, seq_count, group, order),
            out_shape=out_shape,
            in_specs=in_specs,
            out_specs=[vmem()] * len(out_shape),
            scratch_shapes=scratch,
            compiler_params=pltpu.CompilerParams(vmem_limit_bytes=16 << 20),
            cost_estimate=pl.CostEstimate(
                flops=4 * size * block_len * width * hidden_width,
                bytes_accessed=8 << 20,
                transcendentals=size * block_len * hidden_width,
            ),
            name="experts",
        )(exp_index.reshape(1), *weights, *operands)
        return dict(zip(group, zip(outs[:size], outs[size : 2 * size]))), outs[-1]

    there = {"z0": marked}
    near = {}
    for name in SEQUENCE:
        kind, d = name[0], int(name[1])

        def held(value):
            others = [there[other] for other in WAITS.get(name, ())]
            return lax.optimization_barrier((value, *others))[0] if others else value

        if kind == "z":
            there[name] = flipped(held(attended), "seq", d)
        elif kind in "dx":
            there[name] = flipped(held(there[f"z{d}"]), "exp", 1 if kind == "d" else 2)
        elif kind == "e":
            there[name] = flipped(held(there[f"x{d}"]), "exp", 1)
        elif kind == "g":
            group = GROUPS[d]
            marked_blocks = [there[k + "0"] for k in "zdxe"]
            if group[0]:
                last = held(there[f"e{group[0]}"])
            else:
                last = None
                marked_blocks[3] = held(marked_blocks[3])
            outs, extra = experts(group, last)
            if 0 in group:
                own = extra
            for member, (kept, sent) in outs.items():
                there[f"k{member}"], there[f"s{member}"] = kept, sent
            there[name] = there[f"s{group[0]}"]
        elif kind == "r":
            both = there[f"k{d}"].astype(jnp.float32)
            both = both + flipped(held(there[f"s{d}"]), "exp", 1).astype(jnp.float32)
            near[d], there[name] = both[:token_count], both[token_count:].astype(jnp.bfloat16)
        elif kind == "y":
            there[name] = flipped(held(there[f"r{d}"]), "exp", 2)
            near[d] = near[d] + there[name].astype(jnp.float32)
        elif kind == "w":
            there[name] = flipped(held(near[d].astype(jnp.bfloat16)), "seq", d)
            near[d] = there[name].astype(jnp.float32)
    total = jnp.transpose(own, (1, 0, 2)).reshape(token_count, width).astype(jnp.float32)
    for d in sorted(near, reverse=True):
        total = total + near[d]
    return total.astype(jnp.bfloat16)


def solution(mesh):
    placed = (
        P(("dp", "seq"), "exp", None),
        P(("dp", "seq"), "exp", None),
        P(("dp", "seq"), "exp", None),
        P("dp"),
        P(),
        P(("dp", "seq", "exp"), None),
        P(("dp", "seq", "exp"), None),
        P("exp", None, "seq"),
        P("exp", "seq", None),
    )
    small = mesh.shape["seq"] == 4 and mesh.shape["exp"] == 4
    return jax.shard_map(
        gathered_shards if small else routed_shards,
        mesh=mesh,
        in_specs=placed,
        out_specs=P(("dp", "seq", "exp"), None),
        check_vma=False,
    )
```

```python
import functools

import jax
import jax.numpy as jnp
from jax import lax
from jax.experimental import pallas as pl
from jax.experimental.pallas import tpu as pltpu
from jax.sharding import PartitionSpec as P

WINDOW = 2048


epsilon = 1e-05

GROUPS = [[3, 1], [2, 0]]
SEQUENCE = ['z3', 'z1', 'z2', 'd0', 'x3', 'd3', 'x1', 'd1', 'x2', 'd2', 'e1', 'e2', 'x0', 'e0', 'e3', 'g0', 'r1', 'r3', 'g1', 'r2', 'y1', 'r0', 'y3', 'w3', 'y2', 'w2', 'w1', 'y0']
WAITS = {'e0': ('z3',), 'g1': ('r3',), 'r1': ('x1', 'x2'), 'r3': ('x2',), 'y0': ('y2',), 'y1': ('r2',)}


def shifted(x, axis, by):
    size = lax.axis_size(axis)
    pairs = [(i, i + by) for i in range(size) if 0 <= i + by < size]
    return lax.ppermute(x, axis, pairs)


def flipped(x, axis, by):
    return lax.ppermute(x, axis, [(i, i ^ by) for i in range(lax.axis_size(axis))])


def routed_shards(
    queries, keys, values, doc_ids, norm_gain, expert_ids, route_weights, w_in, w_out
):
    block_len, heads_dev, head_dim = queries.shape
    seq_count = lax.axis_size("seq")
    exp_count = lax.axis_size("exp")
    seq_index = lax.axis_index("seq")
    reach_blocks = min(-(-WINDOW // block_len), seq_count - 1)
    own_keys = keys[:, 0, :]
    own_values = values[:, 0, :]
    key_list = [own_keys]
    value_list = [own_values]
    for distance in range(1, reach_blocks + 1):
        far_keys, far_values = shifted((own_keys, own_values), "seq", distance)
        key_list.insert(0, far_keys)
        value_list.insert(0, far_values)
    near_keys = jnp.concatenate(key_list, axis=0)
    near_values = jnp.concatenate(value_list, axis=0)
    key_count = near_keys.shape[0]
    query_rows = jnp.transpose(queries, (1, 0, 2)).reshape(heads_dev * block_len, head_dim)
    score = lax.dot_general(
        query_rows, near_keys, (((1,), (1,)), ((), ())), preferred_element_type=jnp.float32
    )
    score = score * (1.0 / head_dim**0.5)
    query_pos = seq_index * block_len + jnp.arange(block_len, dtype=jnp.int32)
    key_pos = (seq_index - reach_blocks) * block_len + jnp.arange(key_count, dtype=jnp.int32)
    padded_docs = jnp.concatenate(
        [jnp.full((reach_blocks * block_len,), -1, jnp.int32), doc_ids], axis=0
    )
    key_docs = lax.dynamic_slice_in_dim(padded_docs, seq_index * block_len, key_count, 0)
    query_docs = lax.dynamic_slice_in_dim(doc_ids, seq_index * block_len, block_len, 0)
    allowed = (key_pos[None, :] <= query_pos[:, None]) & (
        query_pos[:, None] - key_pos[None, :] < WINDOW
    )
    allowed = allowed & (key_pos[None, :] >= 0) & (query_docs[:, None] == key_docs[None, :])
    allowed = jnp.tile(allowed, (heads_dev, 1))
    score = jnp.where(allowed, score, -jnp.inf)
    top_score = jnp.max(score, axis=1, keepdims=True)
    weights = jnp.where(allowed, jnp.exp(score - top_score), 0.0)
    probs = (weights / jnp.sum(weights, axis=1, keepdims=True)).astype(jnp.bfloat16)
    attended = jnp.dot(probs, near_values, preferred_element_type=jnp.float32).astype(jnp.bfloat16)
    attended = jnp.transpose(attended.reshape(heads_dev, block_len, head_dim), (1, 0, 2)).reshape(
        block_len, heads_dev * head_dim
    )
    attn = lax.all_to_all(attended, "exp", split_axis=0, concat_axis=1, tiled=True)
    token_count = attn.shape[0]
    width = attn.shape[1]
    attn_float = attn.astype(jnp.float32)
    mean_square = jnp.mean(attn_float * attn_float, axis=1, keepdims=True)
    normed = (attn_float * lax.rsqrt(mean_square + epsilon) * norm_gain[None, :]).astype(
        jnp.bfloat16
    )
    capacity = max((token_count + 2) // 3, 2 * token_count // exp_count)
    flat_ids = expert_ids.reshape(token_count * 2)
    onehot = (flat_ids[:, None] == jnp.arange(exp_count, dtype=jnp.int32)[None, :]).astype(
        jnp.int32
    )
    earlier = jnp.cumsum(onehot, axis=0) - onehot
    slot = jnp.sum(earlier * onehot, axis=1)
    local_code = (flat_ids * capacity + slot).reshape(token_count, 2)
    slot_range = jnp.arange(exp_count * capacity, dtype=jnp.int32)
    first_hit = local_code[:, 0:1] == slot_range[None, :]
    second_hit = local_code[:, 1:2] == slot_range[None, :]
    placing = jnp.transpose((first_hit | second_hit).astype(jnp.bfloat16))
    outgoing = jnp.dot(placing, normed, preferred_element_type=jnp.float32).astype(jnp.bfloat16)
    arrived = lax.all_to_all(
        outgoing.reshape(exp_count, capacity, width), "exp", split_axis=0, concat_axis=0, tiled=True
    )
    row_count = exp_count * capacity
    arrived = arrived.reshape(row_count, width)
    weight_in = w_in[0]
    weight_out = w_out[0]
    hidden = jax.nn.silu(
        jnp.dot(
            lax.all_gather(arrived, "seq", axis=0, tiled=True),
            weight_in,
            preferred_element_type=jnp.float32,
        )
    ).astype(jnp.bfloat16)
    summed = lax.psum_scatter(
        jnp.dot(hidden, weight_out, preferred_element_type=jnp.float32).astype(jnp.bfloat16),
        "seq",
        scatter_dimension=0,
        tiled=True,
    )
    expert_out = summed.reshape(exp_count, capacity, width)
    returned = lax.all_to_all(expert_out, "exp", split_axis=0, concat_axis=0, tiled=True).reshape(
        row_count, width
    )
    combine = route_weights[:, 0:1] * first_hit.astype(jnp.float32) + route_weights[
        :, 1:2
    ] * second_hit.astype(jnp.float32)
    moe_part = jnp.dot(
        combine,
        returned.astype(jnp.float32),
        precision=lax.Precision.HIGHEST,
        preferred_element_type=jnp.float32,
    )
    return (attn_float + moe_part).astype(jnp.bfloat16)


def pack_kernel(
    exp_count, keys_ref, values_ref, ids_hbm, route_hbm, out_ref, ids_ref, route_ref, share_ref, sems
):
    block_len = keys_ref.shape[0]
    token_count = ids_ref.shape[1]
    copies = [
        pltpu.make_async_copy(source, target, sems.at[i])
        for i, (source, target) in enumerate(
            [
                (ids_hbm, ids_ref),
                (route_hbm, route_ref),
                (keys_ref, out_ref.at[0:block_len]),
                (values_ref, out_ref.at[block_len : 2 * block_len]),
            ]
        )
    ]
    for copy in copies:
        copy.start()
    share_ref[...] = jnp.zeros_like(share_ref)
    copies[0].wait()
    copies[1].wait()
    for expert in range(exp_count):
        rest = jnp.sum(jnp.where(ids_ref[...] == expert, route_ref[...], 0.0), axis=0, keepdims=True)
        for piece in range(3):
            row = piece * exp_count + expert
            part = rest.astype(jnp.bfloat16).astype(jnp.float32)
            share_ref[row : row + 1, 0:token_count] = part
            rest = rest - part
    out_ref[2 * block_len :] = share_ref[...].astype(jnp.bfloat16)
    copies[2].wait()
    copies[3].wait()


def attend_kernel(block_len, scale, *refs):
    place_ref, query_ref, doc_row, *packs = refs[:-4]
    out_ref, marked_ref, keys_ref, values_ref = refs[-4:]
    place = place_ref[0]
    lanes = packs[0].shape[1]
    for i, pack in enumerate(packs):
        rows = pl.ds(pl.multiple_of((place ^ i) * block_len, block_len), block_len)
        keys_ref[rows] = pack[0:block_len]
        values_ref[rows] = pack[block_len : 2 * block_len]
        marked_ref[block_len:, i * lanes : (i + 1) * lanes] = pack[2 * block_len :]
    marked_ref[block_len:, len(packs) * lanes :] = jnp.zeros(
        (marked_ref.shape[0] - block_len, marked_ref.shape[1] - len(packs) * lanes), jnp.bfloat16
    )
    start = pl.multiple_of(place * block_len, block_len)
    query_pos = start + lax.broadcasted_iota(jnp.int32, (block_len, 1), 0)
    key_pos = lax.broadcasted_iota(jnp.int32, doc_row.shape, 1)
    key_doc = doc_row[...]
    query_doc = jnp.sum(jnp.where(query_pos == key_pos, key_doc, 0), axis=1, keepdims=True)
    allowed = (key_pos <= query_pos) & (query_pos - key_pos < WINDOW) & (query_doc == key_doc)
    head_dim = query_ref.shape[2]
    heads = range(query_ref.shape[0])
    scores = [
        lax.dot_general(
            query_ref[head],
            keys_ref[...],
            (((1,), (1,)), ((), ())),
            preferred_element_type=jnp.float32,
        )
        for head in heads
    ]
    scores = [jnp.where(allowed, score * scale, -jnp.inf) for score in scores]
    tops = [jnp.max(score, axis=1, keepdims=True) for score in scores]
    weights = [jnp.exp(score - top) for score, top in zip(scores, tops)]
    inverses = [1.0 / jnp.sum(weight, axis=1, keepdims=True) for weight in weights]
    for head in heads:
        columns = slice(head * head_dim, (head + 1) * head_dim)
        attended = jnp.dot(
            (weights[head] * inverses[head]).astype(jnp.bfloat16),
            values_ref[...],
            preferred_element_type=jnp.float32,
        ).astype(jnp.bfloat16)
        out_ref[:, columns] = attended
        marked_ref[0:block_len, columns] = attended


def rows_of(part, part_width):
    return pl.ds(pl.multiple_of(part * part_width, part_width), part_width)


def near_kernel(place_ref, w_in_hbm, out_ref, sems):
    place = place_ref[0]
    reads = [
        pltpu.make_async_copy(
            w_in_hbm.at[0, rows_of(place ^ j, out_ref.shape[1])], out_ref.at[j], sems.at[j]
        )
        for j in range(out_ref.shape[0])
    ]
    for read in reads:
        read.start()
    for read in reads:
        read.wait()


def experts_kernel(seq_count, group, order, *refs):
    exp_count = len(order)
    place_ref, gain_hbm, w_in_hbm, w_out_hbm, w_near_ref = refs[:5]
    marked = refs[5 : 5 + exp_count]
    refs = refs[5 + exp_count :]
    blocks = {0: marked}
    for d in group:
        if d:
            blocks[d], refs = refs[:exp_count], refs[exp_count:]
    kept, sent, refs = refs[: len(group)], refs[len(group) : 2 * len(group)], refs[2 * len(group) :]
    if 0 in group:
        own_ref, *refs, split_ref = refs
    hidden_ref, share_ref, gain_ref, w_in_ref, w_out_ref, sum_ref, sems = refs
    place = place_ref[0]
    block_len, token_count = marked[0].shape[0] - 16, hidden_ref.shape[1]
    part_width = marked[0].shape[1]
    width = part_width * exp_count
    lanes = 128

    near_count = w_near_ref.shape[0]
    reads = [
        pltpu.make_async_copy(
            w_in_hbm.at[0, rows_of(place ^ j, part_width)], w_in_ref.at[j - near_count], sems.at[j]
        )
        for j in range(near_count, exp_count)
    ]
    depth = hidden_ref.shape[2] // 2
    reads += [
        pltpu.make_async_copy(
            w_out_hbm.at[0, i * depth : (i + 1) * depth],
            w_out_ref.at[i * depth : (i + 1) * depth],
            sems.at[exp_count + i],
        )
        for i in range(2)
    ]
    reads.insert(0, pltpu.make_async_copy(gain_hbm, gain_ref, sems.at[exp_count + 2]))
    for read in reads:
        read.start()

    share_ref[...] = jnp.zeros_like(share_ref)
    for j in range(exp_count):
        share = marked[j][block_len:].astype(jnp.float32)
        row = lax.broadcasted_iota(jnp.int32, share.shape, 0)
        share = jnp.where(row % exp_count == place, share, 0.0)
        share = jnp.sum(share, axis=0, keepdims=True)
        for i, d in enumerate(group):
            line = i * exp_count + order.index(j)
            share_ref[line : line + 1] = share[:, d * lanes : (d + 1) * lanes]
    share = share_ref[...].T
    weight = jnp.concatenate(
        [share[:token_count, i : i + 1] for i in range(len(group) * exp_count)], axis=0
    )

    reads[0].wait()
    squares = [jnp.zeros((block_len, lanes), jnp.float32)] * len(group)
    hidden = None
    for j in range(exp_count):
        source = place ^ j
        gain = gain_ref[source]
        gained = []
        for i, d in enumerate(group):
            value = blocks[d][j][0:block_len].astype(jnp.float32)
            square = value * value
            for start in range(0, part_width, lanes):
                squares[i] = squares[i] + square[:, start : start + lanes]
            gained.append((value * gain).astype(jnp.bfloat16))
            if d == 0:
                split_ref[...] = value.reshape(exp_count, token_count, part_width)
                own_ref[source] = split_ref[place].astype(jnp.bfloat16)
        if j >= near_count:
            reads[1 + j - near_count].wait()
        w_part = w_near_ref[j] if j < near_count else w_in_ref[j - near_count]
        product = jnp.dot(
            jnp.concatenate(gained, axis=0), w_part, preferred_element_type=jnp.float32
        )
        hidden = product if hidden is None else hidden + product
    mean_square = jnp.sum(jnp.concatenate(squares, axis=0), axis=1, keepdims=True) * (1.0 / width)
    hidden = hidden * lax.rsqrt(mean_square + epsilon)
    hidden = hidden * (1.0 / (1.0 + jnp.exp(-hidden)))
    hidden_ref[...] = hidden.reshape(len(group) * exp_count, token_count, hidden.shape[1])
    hidden = jnp.concatenate(
        [hidden_ref[i * exp_count + (place ^ j)] for i in range(len(group)) for j in order], axis=0
    ).astype(jnp.bfloat16)
    half = block_len // 2
    tiles = [slice(start, start + part_width) for start in range(0, width, part_width)]
    reads[1 + exp_count - near_count].wait()
    for columns in tiles:
        sum_ref[:, columns] = jnp.dot(
            hidden[:, :depth], w_out_ref[:depth, columns], preferred_element_type=jnp.float32
        )
    reads[2 + exp_count - near_count].wait()
    for columns in tiles:
        product = sum_ref[:, columns] + jnp.dot(
            hidden[:, depth:], w_out_ref[depth:, columns], preferred_element_type=jnp.float32
        )
        product = (product * weight).astype(jnp.bfloat16)
        for i in range(len(group)):
            low = i * block_len
            kept[i][:, columns] = product[low : low + half]
            sent[i][:, columns] = product[low + half : low + block_len]


def vmem():
    return pl.BlockSpec(memory_space=pltpu.VMEM)


def anywhere():
    return pl.BlockSpec(memory_space=pltpu.HBM)


def gathered_shards(
    queries, keys, values, doc_ids, norm_gain, expert_ids, route_weights, w_in, w_out
):
    block_len, heads_dev, head_dim = queries.shape
    seq_count = lax.axis_size("seq")
    exp_count = lax.axis_size("exp")
    seq_index = lax.axis_index("seq")
    exp_index = lax.axis_index("exp")
    token_count = expert_ids.shape[0]
    part_width = heads_dev * head_dim
    width = part_width * exp_count
    hidden_width = w_in.shape[2]
    half = block_len // 2
    far = range(1, seq_count)

    pack = pl.pallas_call(
        functools.partial(pack_kernel, exp_count),
        out_shape=jax.ShapeDtypeStruct((2 * block_len + 16, head_dim), jnp.bfloat16),
        in_specs=[anywhere()] * 4,
        out_specs=vmem(),
        scratch_shapes=[
            pltpu.VMEM(expert_ids.shape[::-1], jnp.int32),
            pltpu.VMEM(route_weights.shape[::-1], jnp.float32),
            pltpu.VMEM((16, head_dim), jnp.float32),
            pltpu.SemaphoreType.DMA((4,)),
        ],
        compiler_params=pltpu.CompilerParams(vmem_limit_bytes=4 << 20),
        name="pack",
    )(
        *[
            pltpu.with_memory_space_constraint(x, pltpu.HBM)
            for x in (keys[:, 0, :], values[:, 0, :], expert_ids.T, route_weights.T)
        ]
    )
    packs = [pack] + [flipped(pack, "seq", d) for d in far]

    heads, pack = lax.optimization_barrier((jnp.transpose(queries, (1, 0, 2)), pack))
    heads = heads * jnp.bfloat16(0.125)
    w_in_here, _ = lax.optimization_barrier((w_in, pack))
    w_near = pl.pallas_call(
        near_kernel,
        out_shape=pltpu.VMEM((2, part_width, hidden_width), w_in.dtype),
        in_specs=[pl.BlockSpec(memory_space=pltpu.SMEM), anywhere()],
        out_specs=vmem(),
        scratch_shapes=[pltpu.SemaphoreType.DMA((2,))],
        compiler_params=pltpu.CompilerParams(vmem_limit_bytes=4 << 20),
        name="near",
    )(exp_index.reshape(1), pltpu.with_memory_space_constraint(w_in_here, pltpu.HBM))
    heads, w_near = lax.optimization_barrier((heads, w_near))
    packs[0] = pack

    attended, marked = pl.pallas_call(
        functools.partial(attend_kernel, block_len, 8.0 / head_dim**0.5),
        out_shape=[
            jax.ShapeDtypeStruct((block_len, part_width), jnp.bfloat16),
            jax.ShapeDtypeStruct((block_len + 16, part_width), jnp.bfloat16),
        ],
        in_specs=[pl.BlockSpec(memory_space=pltpu.SMEM)] + [vmem()] * (seq_count + 2),
        out_specs=[vmem()] * 2,
        scratch_shapes=[pltpu.VMEM((seq_count * block_len, head_dim), jnp.bfloat16)] * 2,
        compiler_params=pltpu.CompilerParams(vmem_limit_bytes=8 << 20),
        cost_estimate=pl.CostEstimate(
            flops=4 * heads_dev * block_len * seq_count * block_len * head_dim,
            bytes_accessed=1 << 20,
            transcendentals=heads_dev * block_len * seq_count * block_len,
        ),
        name="attend",
    )(seq_index.reshape(1), heads, doc_ids.reshape(1, -1), *packs)

    order = [j for j in range(exp_count) if not j & 1] + [j for j in range(exp_count) if j & 1]
    gain = norm_gain.reshape(exp_count, 1, part_width)
    weights = [pltpu.with_memory_space_constraint(w, pltpu.HBM) for w in (gain, w_in, w_out)]

    def experts(group, last):
        size = len(group)
        operands = list(marked_blocks)
        for d in group:
            if d:
                operands += [there[kind + str(d)] for kind in "zdx"]
                operands.append(there["e" + str(d)] if d != group[0] else last)
        out_shape = [jax.ShapeDtypeStruct((half, width), jnp.bfloat16)] * (2 * size)
        scratch = [
            pltpu.VMEM((size * exp_count, token_count, hidden_width), jnp.float32),
            pltpu.VMEM((head_dim, head_dim), jnp.float32),
            pltpu.VMEM((exp_count, 1, part_width), jnp.float32),
            pltpu.VMEM((exp_count - w_near.shape[0], part_width, hidden_width), jnp.bfloat16),
            pltpu.VMEM((hidden_width, width), jnp.bfloat16),
            pltpu.VMEM((size * block_len, width), jnp.float32),
            pltpu.SemaphoreType.DMA((exp_count + 3,)),
        ]
        if 0 in group:
            split = (exp_count, token_count, part_width)
            out_shape.append(jax.ShapeDtypeStruct(split, jnp.bfloat16))
            scratch.append(pltpu.VMEM(split, jnp.float32))
        in_specs = [pl.BlockSpec(memory_space=pltpu.SMEM)] + [vmem()] * (4 + len(operands))
        in_specs[1:4] = [anywhere()] * 3
        outs = pl.pallas_call(
            functools.partial(experts_kernel, seq_count, group, order),
            out_shape=out_shape,
            in_specs=in_specs,
            out_specs=[vmem()] * len(out_shape),
            scratch_shapes=scratch,
            compiler_params=pltpu.CompilerParams(vmem_limit_bytes=16 << 20),
            cost_estimate=pl.CostEstimate(
                flops=4 * size * block_len * width * hidden_width,
                bytes_accessed=8 << 20,
                transcendentals=size * block_len * hidden_width,
            ),
            name="experts",
        )(exp_index.reshape(1), *weights, w_near, *operands)
        return dict(zip(group, zip(outs[:size], outs[size : 2 * size]))), outs[-1]

    there = {"z0": marked}
    near = {}
    for name in SEQUENCE:
        kind, d = name[0], int(name[1])

        def held(value):
            others = [there[other] for other in WAITS.get(name, ())]
            return lax.optimization_barrier((value, *others))[0] if others else value

        if kind == "z":
            there[name] = flipped(held(attended), "seq", d)
        elif kind in "dx":
            there[name] = flipped(held(there[f"z{d}"]), "exp", 1 if kind == "d" else 2)
        elif kind == "e":
            there[name] = flipped(held(there[f"x{d}"]), "exp", 1)
        elif kind == "g":
            group = GROUPS[d]
            marked_blocks = [there[k + "0"] for k in "zdxe"]
            if group[0]:
                last = held(there[f"e{group[0]}"])
            else:
                last = None
                marked_blocks[3] = held(marked_blocks[3])
            outs, extra = experts(group, last)
            if 0 in group:
                own = extra
            for member, (kept, sent) in outs.items():
                there[f"k{member}"], there[f"s{member}"] = kept, sent
            there[name] = there[f"s{group[0]}"]
        elif kind == "r":
            both = there[f"k{d}"].astype(jnp.float32)
            both = both + flipped(held(there[f"s{d}"]), "exp", 1).astype(jnp.float32)
            near[d], there[name] = both[:token_count], both[token_count:].astype(jnp.bfloat16)
        elif kind == "y":
            there[name] = flipped(held(there[f"r{d}"]), "exp", 2)
            near[d] = near[d] + there[name].astype(jnp.float32)
        elif kind == "w":
            there[name] = flipped(held(near[d].astype(jnp.bfloat16)), "seq", d)
            near[d] = there[name].astype(jnp.float32)
    total = jnp.transpose(own, (1, 0, 2)).reshape(token_count, width).astype(jnp.float32)
    for d in sorted(near, reverse=True):
        total = total + near[d]
    return total.astype(jnp.bfloat16)


def solution(mesh):
    placed = (
        P(("dp", "seq"), "exp", None),
        P(("dp", "seq"), "exp", None),
        P(("dp", "seq"), "exp", None),
        P("dp"),
        P(),
        P(("dp", "seq", "exp"), None),
        P(("dp", "seq", "exp"), None),
        P("exp", None, "seq"),
        P("exp", "seq", None),
    )
    small = mesh.shape["seq"] == 4 and mesh.shape["exp"] == 4
    return jax.shard_map(
        gathered_shards if small else routed_shards,
        mesh=mesh,
        in_specs=placed,
        out_specs=P(("dp", "seq", "exp"), None),
        check_vma=False,
    )
```

```python
import functools

import jax
import jax.numpy as jnp
from jax import lax
from jax.experimental import pallas as pl
from jax.experimental.pallas import tpu as pltpu
from jax.sharding import PartitionSpec as P

WINDOW = 2048


epsilon = 1e-05

GROUPS = [[3, 1], [2, 0]]
SEQUENCE = ['z3', 'z1', 'z2', 'd0', 'x3', 'd3', 'x1', 'd1', 'x2', 'd2', 'e1', 'e2', 'x0', 'e0', 'e3', 'g0', 'r3', 'r1', 'g1', 'r2', 'y1', 'r0', 'y3', 'w3', 'y2', 'w2', 'w1', 'y0']
WAITS = {'d3': ('z1',), 'e0': ('z3',), 'e2': ('x3',), 'g1': ('r3',), 'r1': ('x2',), 'r3': ('x2',), 'y0': ('y2',), 'y1': ('r2',)}


def shifted(x, axis, by):
    size = lax.axis_size(axis)
    pairs = [(i, i + by) for i in range(size) if 0 <= i + by < size]
    return lax.ppermute(x, axis, pairs)


def flipped(x, axis, by):
    return lax.ppermute(x, axis, [(i, i ^ by) for i in range(lax.axis_size(axis))])


def routed_shards(
    queries, keys, values, doc_ids, norm_gain, expert_ids, route_weights, w_in, w_out
):
    block_len, heads_dev, head_dim = queries.shape
    seq_count = lax.axis_size("seq")
    exp_count = lax.axis_size("exp")
    seq_index = lax.axis_index("seq")
    reach_blocks = min(-(-WINDOW // block_len), seq_count - 1)
    own_keys = keys[:, 0, :]
    own_values = values[:, 0, :]
    key_list = [own_keys]
    value_list = [own_values]
    for distance in range(1, reach_blocks + 1):
        far_keys, far_values = shifted((own_keys, own_values), "seq", distance)
        key_list.insert(0, far_keys)
        value_list.insert(0, far_values)
    near_keys = jnp.concatenate(key_list, axis=0)
    near_values = jnp.concatenate(value_list, axis=0)
    key_count = near_keys.shape[0]
    query_rows = jnp.transpose(queries, (1, 0, 2)).reshape(heads_dev * block_len, head_dim)
    score = lax.dot_general(
        query_rows, near_keys, (((1,), (1,)), ((), ())), preferred_element_type=jnp.float32
    )
    score = score * (1.0 / head_dim**0.5)
    query_pos = seq_index * block_len + jnp.arange(block_len, dtype=jnp.int32)
    key_pos = (seq_index - reach_blocks) * block_len + jnp.arange(key_count, dtype=jnp.int32)
    padded_docs = jnp.concatenate(
        [jnp.full((reach_blocks * block_len,), -1, jnp.int32), doc_ids], axis=0
    )
    key_docs = lax.dynamic_slice_in_dim(padded_docs, seq_index * block_len, key_count, 0)
    query_docs = lax.dynamic_slice_in_dim(doc_ids, seq_index * block_len, block_len, 0)
    allowed = (key_pos[None, :] <= query_pos[:, None]) & (
        query_pos[:, None] - key_pos[None, :] < WINDOW
    )
    allowed = allowed & (key_pos[None, :] >= 0) & (query_docs[:, None] == key_docs[None, :])
    allowed = jnp.tile(allowed, (heads_dev, 1))
    score = jnp.where(allowed, score, -jnp.inf)
    top_score = jnp.max(score, axis=1, keepdims=True)
    weights = jnp.where(allowed, jnp.exp(score - top_score), 0.0)
    probs = (weights / jnp.sum(weights, axis=1, keepdims=True)).astype(jnp.bfloat16)
    attended = jnp.dot(probs, near_values, preferred_element_type=jnp.float32).astype(jnp.bfloat16)
    attended = jnp.transpose(attended.reshape(heads_dev, block_len, head_dim), (1, 0, 2)).reshape(
        block_len, heads_dev * head_dim
    )
    attn = lax.all_to_all(attended, "exp", split_axis=0, concat_axis=1, tiled=True)
    token_count = attn.shape[0]
    width = attn.shape[1]
    attn_float = attn.astype(jnp.float32)
    mean_square = jnp.mean(attn_float * attn_float, axis=1, keepdims=True)
    normed = (attn_float * lax.rsqrt(mean_square + epsilon) * norm_gain[None, :]).astype(
        jnp.bfloat16
    )
    capacity = max((token_count + 2) // 3, 2 * token_count // exp_count)
    flat_ids = expert_ids.reshape(token_count * 2)
    onehot = (flat_ids[:, None] == jnp.arange(exp_count, dtype=jnp.int32)[None, :]).astype(
        jnp.int32
    )
    earlier = jnp.cumsum(onehot, axis=0) - onehot
    slot = jnp.sum(earlier * onehot, axis=1)
    local_code = (flat_ids * capacity + slot).reshape(token_count, 2)
    slot_range = jnp.arange(exp_count * capacity, dtype=jnp.int32)
    first_hit = local_code[:, 0:1] == slot_range[None, :]
    second_hit = local_code[:, 1:2] == slot_range[None, :]
    placing = jnp.transpose((first_hit | second_hit).astype(jnp.bfloat16))
    outgoing = jnp.dot(placing, normed, preferred_element_type=jnp.float32).astype(jnp.bfloat16)
    arrived = lax.all_to_all(
        outgoing.reshape(exp_count, capacity, width), "exp", split_axis=0, concat_axis=0, tiled=True
    )
    row_count = exp_count * capacity
    arrived = arrived.reshape(row_count, width)
    weight_in = w_in[0]
    weight_out = w_out[0]
    hidden = jax.nn.silu(
        jnp.dot(
            lax.all_gather(arrived, "seq", axis=0, tiled=True),
            weight_in,
            preferred_element_type=jnp.float32,
        )
    ).astype(jnp.bfloat16)
    summed = lax.psum_scatter(
        jnp.dot(hidden, weight_out, preferred_element_type=jnp.float32).astype(jnp.bfloat16),
        "seq",
        scatter_dimension=0,
        tiled=True,
    )
    expert_out = summed.reshape(exp_count, capacity, width)
    returned = lax.all_to_all(expert_out, "exp", split_axis=0, concat_axis=0, tiled=True).reshape(
        row_count, width
    )
    combine = route_weights[:, 0:1] * first_hit.astype(jnp.float32) + route_weights[
        :, 1:2
    ] * second_hit.astype(jnp.float32)
    moe_part = jnp.dot(
        combine,
        returned.astype(jnp.float32),
        precision=lax.Precision.HIGHEST,
        preferred_element_type=jnp.float32,
    )
    return (attn_float + moe_part).astype(jnp.bfloat16)


def pack_kernel(
    exp_count, keys_ref, values_ref, ids_hbm, route_hbm, out_ref, ids_ref, route_ref, share_ref, sems
):
    block_len = keys_ref.shape[0]
    token_count = ids_ref.shape[1]
    copies = [
        pltpu.make_async_copy(source, target, sems.at[i])
        for i, (source, target) in enumerate(
            [
                (ids_hbm, ids_ref),
                (route_hbm, route_ref),
                (keys_ref, out_ref.at[0:block_len]),
                (values_ref, out_ref.at[block_len : 2 * block_len]),
            ]
        )
    ]
    for copy in copies:
        copy.start()
    share_ref[...] = jnp.zeros_like(share_ref)
    copies[0].wait()
    copies[1].wait()
    for expert in range(exp_count):
        rest = jnp.sum(jnp.where(ids_ref[...] == expert, route_ref[...], 0.0), axis=0, keepdims=True)
        for piece in range(3):
            row = piece * exp_count + expert
            part = rest.astype(jnp.bfloat16).astype(jnp.float32)
            share_ref[row : row + 1, 0:token_count] = part
            rest = rest - part
    out_ref[2 * block_len :] = share_ref[...].astype(jnp.bfloat16)
    copies[2].wait()
    copies[3].wait()


def attend_kernel(block_len, scale, *refs):
    place_ref, query_ref, doc_row, *packs = refs[:-4]
    out_ref, marked_ref, keys_ref, values_ref = refs[-4:]
    place = place_ref[0]
    lanes = packs[0].shape[1]
    for i, pack in enumerate(packs):
        rows = pl.ds(pl.multiple_of((place ^ i) * block_len, block_len), block_len)
        keys_ref[rows] = pack[0:block_len]
        values_ref[rows] = pack[block_len : 2 * block_len]
        marked_ref[block_len:, i * lanes : (i + 1) * lanes] = pack[2 * block_len :]
    marked_ref[block_len:, len(packs) * lanes :] = jnp.zeros(
        (marked_ref.shape[0] - block_len, marked_ref.shape[1] - len(packs) * lanes), jnp.bfloat16
    )
    start = pl.multiple_of(place * block_len, block_len)
    query_pos = start + lax.broadcasted_iota(jnp.int32, (block_len, 1), 0)
    key_pos = lax.broadcasted_iota(jnp.int32, doc_row.shape, 1)
    key_doc = doc_row[...]
    query_doc = jnp.sum(jnp.where(query_pos == key_pos, key_doc, 0), axis=1, keepdims=True)
    allowed = (key_pos <= query_pos) & (query_pos - key_pos < WINDOW) & (query_doc == key_doc)
    head_dim = query_ref.shape[2]
    heads = range(query_ref.shape[0])
    scores = [
        lax.dot_general(
            query_ref[head],
            keys_ref[...],
            (((1,), (1,)), ((), ())),
            preferred_element_type=jnp.float32,
        )
        for head in heads
    ]
    scores = [jnp.where(allowed, score * scale, -jnp.inf) for score in scores]
    tops = [jnp.max(score, axis=1, keepdims=True) for score in scores]
    weights = [jnp.exp(score - top) for score, top in zip(scores, tops)]
    inverses = [1.0 / jnp.sum(weight, axis=1, keepdims=True) for weight in weights]
    for head in heads:
        columns = slice(head * head_dim, (head + 1) * head_dim)
        attended = jnp.dot(
            (weights[head] * inverses[head]).astype(jnp.bfloat16),
            values_ref[...],
            preferred_element_type=jnp.float32,
        ).astype(jnp.bfloat16)
        out_ref[:, columns] = attended
        marked_ref[0:block_len, columns] = attended


def rows_of(part, part_width):
    return pl.ds(pl.multiple_of(part * part_width, part_width), part_width)


def near_kernel(place_ref, w_in_hbm, out_ref, sems):
    place = place_ref[0]
    reads = [
        pltpu.make_async_copy(
            w_in_hbm.at[0, rows_of(place ^ j, out_ref.shape[1])], out_ref.at[j], sems.at[j]
        )
        for j in range(out_ref.shape[0])
    ]
    for read in reads:
        read.start()
    for read in reads:
        read.wait()


def experts_kernel(seq_count, group, order, *refs):
    exp_count = len(order)
    place_ref, gain_hbm, w_in_hbm, w_out_hbm, w_near_ref = refs[:5]
    marked = refs[5 : 5 + exp_count]
    refs = refs[5 + exp_count :]
    blocks = {0: marked}
    for d in group:
        if d:
            blocks[d], refs = refs[:exp_count], refs[exp_count:]
    kept, sent, refs = refs[: len(group)], refs[len(group) : 2 * len(group)], refs[2 * len(group) :]
    if 0 in group:
        own_ref, *refs, split_ref = refs
    hidden_ref, share_ref, gain_ref, w_in_ref, w_out_ref, sum_ref, sems = refs
    place = place_ref[0]
    block_len, token_count = marked[0].shape[0] - 16, hidden_ref.shape[1]
    part_width = marked[0].shape[1]
    width = part_width * exp_count
    lanes = 128

    near_count = w_near_ref.shape[0]
    reads = [
        pltpu.make_async_copy(
            w_in_hbm.at[0, rows_of(place ^ j, part_width)], w_in_ref.at[j - near_count], sems.at[j]
        )
        for j in range(near_count, exp_count)
    ]
    depth = hidden_ref.shape[2] // 2
    reads += [
        pltpu.make_async_copy(
            w_out_hbm.at[0, i * depth : (i + 1) * depth],
            w_out_ref.at[i * depth : (i + 1) * depth],
            sems.at[exp_count + i],
        )
        for i in range(2)
    ]
    reads.insert(0, pltpu.make_async_copy(gain_hbm, gain_ref, sems.at[exp_count + 2]))
    for read in reads:
        read.start()

    share_ref[...] = jnp.zeros_like(share_ref)
    for j in range(exp_count):
        share = marked[j][block_len:].astype(jnp.float32)
        row = lax.broadcasted_iota(jnp.int32, share.shape, 0)
        share = jnp.where(row % exp_count == place, share, 0.0)
        share = jnp.sum(share, axis=0, keepdims=True)
        for i, d in enumerate(group):
            line = i * exp_count + order.index(j)
            share_ref[line : line + 1] = share[:, d * lanes : (d + 1) * lanes]
    share = share_ref[...].T
    weight = jnp.concatenate(
        [share[:token_count, i : i + 1] for i in range(len(group) * exp_count)], axis=0
    )

    reads[0].wait()
    squares = [jnp.zeros((block_len, lanes), jnp.float32)] * len(group)
    hidden = None
    for j in range(exp_count):
        source = place ^ j
        gain = gain_ref[source]
        gained = []
        for i, d in enumerate(group):
            value = blocks[d][j][0:block_len].astype(jnp.float32)
            square = value * value
            for start in range(0, part_width, lanes):
                squares[i] = squares[i] + square[:, start : start + lanes]
            gained.append((value * gain).astype(jnp.bfloat16))
            if d == 0:
                split_ref[...] = value.reshape(exp_count, token_count, part_width)
                own_ref[source] = split_ref[place].astype(jnp.bfloat16)
        if j >= near_count:
            reads[1 + j - near_count].wait()
        w_part = w_near_ref[j] if j < near_count else w_in_ref[j - near_count]
        product = jnp.dot(
            jnp.concatenate(gained, axis=0), w_part, preferred_element_type=jnp.float32
        )
        hidden = product if hidden is None else hidden + product
    mean_square = jnp.sum(jnp.concatenate(squares, axis=0), axis=1, keepdims=True) * (1.0 / width)
    hidden = hidden * lax.rsqrt(mean_square + epsilon)
    hidden = hidden * (1.0 / (1.0 + jnp.exp(-hidden)))
    hidden_ref[...] = hidden.reshape(len(group) * exp_count, token_count, hidden.shape[1])
    hidden = jnp.concatenate(
        [hidden_ref[i * exp_count + (place ^ j)] for i in range(len(group)) for j in order], axis=0
    ).astype(jnp.bfloat16)
    half = block_len // 2
    tiles = [slice(start, start + part_width) for start in range(0, width, part_width)]
    reads[1 + exp_count - near_count].wait()
    for columns in tiles:
        sum_ref[:, columns] = jnp.dot(
            hidden[:, :depth], w_out_ref[:depth, columns], preferred_element_type=jnp.float32
        )
    reads[2 + exp_count - near_count].wait()
    for columns in tiles:
        product = sum_ref[:, columns] + jnp.dot(
            hidden[:, depth:], w_out_ref[depth:, columns], preferred_element_type=jnp.float32
        )
        product = (product * weight).astype(jnp.bfloat16)
        for i in range(len(group)):
            low = i * block_len
            kept[i][:, columns] = product[low : low + half]
            sent[i][:, columns] = product[low + half : low + block_len]


def vmem():
    return pl.BlockSpec(memory_space=pltpu.VMEM)


def anywhere():
    return pl.BlockSpec(memory_space=pltpu.HBM)


def gathered_shards(
    queries, keys, values, doc_ids, norm_gain, expert_ids, route_weights, w_in, w_out
):
    block_len, heads_dev, head_dim = queries.shape
    seq_count = lax.axis_size("seq")
    exp_count = lax.axis_size("exp")
    seq_index = lax.axis_index("seq")
    exp_index = lax.axis_index("exp")
    token_count = expert_ids.shape[0]
    part_width = heads_dev * head_dim
    width = part_width * exp_count
    hidden_width = w_in.shape[2]
    half = block_len // 2
    far = range(1, seq_count)

    pack = pl.pallas_call(
        functools.partial(pack_kernel, exp_count),
        out_shape=jax.ShapeDtypeStruct((2 * block_len + 16, head_dim), jnp.bfloat16),
        in_specs=[anywhere()] * 4,
        out_specs=vmem(),
        scratch_shapes=[
            pltpu.VMEM(expert_ids.shape[::-1], jnp.int32),
            pltpu.VMEM(route_weights.shape[::-1], jnp.float32),
            pltpu.VMEM((16, head_dim), jnp.float32),
            pltpu.SemaphoreType.DMA((4,)),
        ],
        compiler_params=pltpu.CompilerParams(vmem_limit_bytes=4 << 20),
        name="pack",
    )(
        *[
            pltpu.with_memory_space_constraint(x, pltpu.HBM)
            for x in (keys[:, 0, :], values[:, 0, :], expert_ids.T, route_weights.T)
        ]
    )
    packs = [pack] + [flipped(pack, "seq", d) for d in far]

    heads, pack = lax.optimization_barrier((jnp.transpose(queries, (1, 0, 2)), pack))
    heads = heads * jnp.bfloat16(0.125)
    w_in_here, _ = lax.optimization_barrier((w_in, pack))
    w_near = pl.pallas_call(
        near_kernel,
        out_shape=pltpu.VMEM((3, part_width, hidden_width), w_in.dtype),
        in_specs=[pl.BlockSpec(memory_space=pltpu.SMEM), anywhere()],
        out_specs=vmem(),
        scratch_shapes=[pltpu.SemaphoreType.DMA((3,))],
        compiler_params=pltpu.CompilerParams(vmem_limit_bytes=4 << 20),
        name="near",
    )(exp_index.reshape(1), pltpu.with_memory_space_constraint(w_in_here, pltpu.HBM))
    heads, w_near = lax.optimization_barrier((heads, w_near))
    packs[0] = pack

    attended, marked = pl.pallas_call(
        functools.partial(attend_kernel, block_len, 8.0 / head_dim**0.5),
        out_shape=[
            jax.ShapeDtypeStruct((block_len, part_width), jnp.bfloat16),
            jax.ShapeDtypeStruct((block_len + 16, part_width), jnp.bfloat16),
        ],
        in_specs=[pl.BlockSpec(memory_space=pltpu.SMEM)] + [vmem()] * (seq_count + 2),
        out_specs=[vmem()] * 2,
        scratch_shapes=[pltpu.VMEM((seq_count * block_len, head_dim), jnp.bfloat16)] * 2,
        compiler_params=pltpu.CompilerParams(vmem_limit_bytes=8 << 20),
        cost_estimate=pl.CostEstimate(
            flops=4 * heads_dev * block_len * seq_count * block_len * head_dim,
            bytes_accessed=1 << 20,
            transcendentals=heads_dev * block_len * seq_count * block_len,
        ),
        name="attend",
    )(seq_index.reshape(1), heads, doc_ids.reshape(1, -1), *packs)

    order = [j for j in range(exp_count) if not j & 1] + [j for j in range(exp_count) if j & 1]
    gain = norm_gain.reshape(exp_count, 1, part_width)
    weights = [pltpu.with_memory_space_constraint(w, pltpu.HBM) for w in (gain, w_in, w_out)]

    def experts(group, last):
        size = len(group)
        operands = list(marked_blocks)
        for d in group:
            if d:
                operands += [there[kind + str(d)] for kind in "zdx"]
                operands.append(there["e" + str(d)] if d != group[0] else last)
        out_shape = [jax.ShapeDtypeStruct((half, width), jnp.bfloat16)] * (2 * size)
        scratch = [
            pltpu.VMEM((size * exp_count, token_count, hidden_width), jnp.float32),
            pltpu.VMEM((head_dim, head_dim), jnp.float32),
            pltpu.VMEM((exp_count, 1, part_width), jnp.float32),
            pltpu.VMEM((exp_count - w_near.shape[0], part_width, hidden_width), jnp.bfloat16),
            pltpu.VMEM((hidden_width, width), jnp.bfloat16),
            pltpu.VMEM((size * block_len, width), jnp.float32),
            pltpu.SemaphoreType.DMA((exp_count + 3,)),
        ]
        if 0 in group:
            split = (exp_count, token_count, part_width)
            out_shape.append(jax.ShapeDtypeStruct(split, jnp.bfloat16))
            scratch.append(pltpu.VMEM(split, jnp.float32))
        in_specs = [pl.BlockSpec(memory_space=pltpu.SMEM)] + [vmem()] * (4 + len(operands))
        in_specs[1:4] = [anywhere()] * 3
        outs = pl.pallas_call(
            functools.partial(experts_kernel, seq_count, group, order),
            out_shape=out_shape,
            in_specs=in_specs,
            out_specs=[vmem()] * len(out_shape),
            scratch_shapes=scratch,
            compiler_params=pltpu.CompilerParams(vmem_limit_bytes=16 << 20),
            cost_estimate=pl.CostEstimate(
                flops=4 * size * block_len * width * hidden_width,
                bytes_accessed=8 << 20,
                transcendentals=size * block_len * hidden_width,
            ),
            name="experts",
        )(exp_index.reshape(1), *weights, w_near, *operands)
        return dict(zip(group, zip(outs[:size], outs[size : 2 * size]))), outs[-1]

    there = {"z0": marked}
    near = {}
    for name in SEQUENCE:
        kind, d = name[0], int(name[1])

        def held(value):
            others = [there[other] for other in WAITS.get(name, ())]
            return lax.optimization_barrier((value, *others))[0] if others else value

        if kind == "z":
            there[name] = flipped(held(attended), "seq", d)
        elif kind in "dx":
            there[name] = flipped(held(there[f"z{d}"]), "exp", 1 if kind == "d" else 2)
        elif kind == "e":
            there[name] = flipped(held(there[f"x{d}"]), "exp", 1)
        elif kind == "g":
            group = GROUPS[d]
            marked_blocks = [there[k + "0"] for k in "zdxe"]
            if group[0]:
                last = held(there[f"e{group[0]}"])
            else:
                last = None
                marked_blocks[3] = held(marked_blocks[3])
            outs, extra = experts(group, last)
            if 0 in group:
                own = extra
            for member, (kept, sent) in outs.items():
                there[f"k{member}"], there[f"s{member}"] = kept, sent
            there[name] = there[f"s{group[0]}"]
        elif kind == "r":
            both = there[f"k{d}"].astype(jnp.float32)
            both = both + flipped(held(there[f"s{d}"]), "exp", 1).astype(jnp.float32)
            near[d], there[name] = both[:token_count], both[token_count:].astype(jnp.bfloat16)
        elif kind == "y":
            there[name] = flipped(held(there[f"r{d}"]), "exp", 2)
            near[d] = near[d] + there[name].astype(jnp.float32)
        elif kind == "w":
            there[name] = flipped(held(near[d].astype(jnp.bfloat16)), "seq", d)
            near[d] = there[name].astype(jnp.float32)
    total = jnp.transpose(own, (1, 0, 2)).reshape(token_count, width).astype(jnp.float32)
    for d in sorted(near, reverse=True):
        total = total + near[d]
    return total.astype(jnp.bfloat16)


def solution(mesh):
    placed = (
        P(("dp", "seq"), "exp", None),
        P(("dp", "seq"), "exp", None),
        P(("dp", "seq"), "exp", None),
        P("dp"),
        P(),
        P(("dp", "seq", "exp"), None),
        P(("dp", "seq", "exp"), None),
        P("exp", None, "seq"),
        P("exp", "seq", None),
    )
    small = mesh.shape["seq"] == 4 and mesh.shape["exp"] == 4
    return jax.shard_map(
        gathered_shards if small else routed_shards,
        mesh=mesh,
        in_specs=placed,
        out_specs=P(("dp", "seq", "exp"), None),
        check_vma=False,
    )
```

```python
import functools

import jax
import jax.numpy as jnp
from jax import lax
from jax.experimental import pallas as pl
from jax.experimental.pallas import tpu as pltpu
from jax.sharding import PartitionSpec as P

WINDOW = 2048


epsilon = 1e-05

GROUPS = [[3, 1], [2, 0]]
SEQUENCE = ['z3', 'z1', 'z2', 'd0', 'x3', 'd3', 'x1', 'd1', 'x2', 'd2', 'e1', 'e2', 'x0', 'e0', 'e3', 'g0', 'r3', 'r1', 'g1', 'r2', 'y1', 'r0', 'y3', 'w3', 'y2', 'w2', 'w1', 'y0']
WAITS = {'d3': ('z1',), 'e0': ('z3',), 'e2': ('x3',), 'g1': ('r3',), 'r3': ('x2',), 'y0': ('y2',), 'y1': ('r2',)}


def shifted(x, axis, by):
    size = lax.axis_size(axis)
    pairs = [(i, i + by) for i in range(size) if 0 <= i + by < size]
    return lax.ppermute(x, axis, pairs)


def flipped(x, axis, by):
    return lax.ppermute(x, axis, [(i, i ^ by) for i in range(lax.axis_size(axis))])


def routed_shards(
    queries, keys, values, doc_ids, norm_gain, expert_ids, route_weights, w_in, w_out
):
    block_len, heads_dev, head_dim = queries.shape
    seq_count = lax.axis_size("seq")
    exp_count = lax.axis_size("exp")
    seq_index = lax.axis_index("seq")
    reach_blocks = min(-(-WINDOW // block_len), seq_count - 1)
    own_keys = keys[:, 0, :]
    own_values = values[:, 0, :]
    key_list = [own_keys]
    value_list = [own_values]
    for distance in range(1, reach_blocks + 1):
        far_keys, far_values = shifted((own_keys, own_values), "seq", distance)
        key_list.insert(0, far_keys)
        value_list.insert(0, far_values)
    near_keys = jnp.concatenate(key_list, axis=0)
    near_values = jnp.concatenate(value_list, axis=0)
    key_count = near_keys.shape[0]
    query_rows = jnp.transpose(queries, (1, 0, 2)).reshape(heads_dev * block_len, head_dim)
    score = lax.dot_general(
        query_rows, near_keys, (((1,), (1,)), ((), ())), preferred_element_type=jnp.float32
    )
    score = score * (1.0 / head_dim**0.5)
    query_pos = seq_index * block_len + jnp.arange(block_len, dtype=jnp.int32)
    key_pos = (seq_index - reach_blocks) * block_len + jnp.arange(key_count, dtype=jnp.int32)
    padded_docs = jnp.concatenate(
        [jnp.full((reach_blocks * block_len,), -1, jnp.int32), doc_ids], axis=0
    )
    key_docs = lax.dynamic_slice_in_dim(padded_docs, seq_index * block_len, key_count, 0)
    query_docs = lax.dynamic_slice_in_dim(doc_ids, seq_index * block_len, block_len, 0)
    allowed = (key_pos[None, :] <= query_pos[:, None]) & (
        query_pos[:, None] - key_pos[None, :] < WINDOW
    )
    allowed = allowed & (key_pos[None, :] >= 0) & (query_docs[:, None] == key_docs[None, :])
    allowed = jnp.tile(allowed, (heads_dev, 1))
    score = jnp.where(allowed, score, -jnp.inf)
    top_score = jnp.max(score, axis=1, keepdims=True)
    weights = jnp.where(allowed, jnp.exp(score - top_score), 0.0)
    probs = (weights / jnp.sum(weights, axis=1, keepdims=True)).astype(jnp.bfloat16)
    attended = jnp.dot(probs, near_values, preferred_element_type=jnp.float32).astype(jnp.bfloat16)
    attended = jnp.transpose(attended.reshape(heads_dev, block_len, head_dim), (1, 0, 2)).reshape(
        block_len, heads_dev * head_dim
    )
    attn = lax.all_to_all(attended, "exp", split_axis=0, concat_axis=1, tiled=True)
    token_count = attn.shape[0]
    width = attn.shape[1]
    attn_float = attn.astype(jnp.float32)
    mean_square = jnp.mean(attn_float * attn_float, axis=1, keepdims=True)
    normed = (attn_float * lax.rsqrt(mean_square + epsilon) * norm_gain[None, :]).astype(
        jnp.bfloat16
    )
    capacity = max((token_count + 2) // 3, 2 * token_count // exp_count)
    flat_ids = expert_ids.reshape(token_count * 2)
    onehot = (flat_ids[:, None] == jnp.arange(exp_count, dtype=jnp.int32)[None, :]).astype(
        jnp.int32
    )
    earlier = jnp.cumsum(onehot, axis=0) - onehot
    slot = jnp.sum(earlier * onehot, axis=1)
    local_code = (flat_ids * capacity + slot).reshape(token_count, 2)
    slot_range = jnp.arange(exp_count * capacity, dtype=jnp.int32)
    first_hit = local_code[:, 0:1] == slot_range[None, :]
    second_hit = local_code[:, 1:2] == slot_range[None, :]
    placing = jnp.transpose((first_hit | second_hit).astype(jnp.bfloat16))
    outgoing = jnp.dot(placing, normed, preferred_element_type=jnp.float32).astype(jnp.bfloat16)
    arrived = lax.all_to_all(
        outgoing.reshape(exp_count, capacity, width), "exp", split_axis=0, concat_axis=0, tiled=True
    )
    row_count = exp_count * capacity
    arrived = arrived.reshape(row_count, width)
    weight_in = w_in[0]
    weight_out = w_out[0]
    hidden = jax.nn.silu(
        jnp.dot(
            lax.all_gather(arrived, "seq", axis=0, tiled=True),
            weight_in,
            preferred_element_type=jnp.float32,
        )
    ).astype(jnp.bfloat16)
    summed = lax.psum_scatter(
        jnp.dot(hidden, weight_out, preferred_element_type=jnp.float32).astype(jnp.bfloat16),
        "seq",
        scatter_dimension=0,
        tiled=True,
    )
    expert_out = summed.reshape(exp_count, capacity, width)
    returned = lax.all_to_all(expert_out, "exp", split_axis=0, concat_axis=0, tiled=True).reshape(
        row_count, width
    )
    combine = route_weights[:, 0:1] * first_hit.astype(jnp.float32) + route_weights[
        :, 1:2
    ] * second_hit.astype(jnp.float32)
    moe_part = jnp.dot(
        combine,
        returned.astype(jnp.float32),
        precision=lax.Precision.HIGHEST,
        preferred_element_type=jnp.float32,
    )
    return (attn_float + moe_part).astype(jnp.bfloat16)


def pack_kernel(
    exp_count, keys_ref, values_ref, ids_hbm, route_hbm, out_ref, ids_ref, route_ref, share_ref, sems
):
    block_len = keys_ref.shape[0]
    token_count = ids_ref.shape[1]
    copies = [
        pltpu.make_async_copy(source, target, sems.at[i])
        for i, (source, target) in enumerate(
            [
                (ids_hbm, ids_ref),
                (route_hbm, route_ref),
                (keys_ref, out_ref.at[0:block_len]),
                (values_ref, out_ref.at[block_len : 2 * block_len]),
            ]
        )
    ]
    for copy in copies:
        copy.start()
    share_ref[...] = jnp.zeros_like(share_ref)
    copies[0].wait()
    copies[1].wait()
    for expert in range(exp_count):
        rest = jnp.sum(jnp.where(ids_ref[...] == expert, route_ref[...], 0.0), axis=0, keepdims=True)
        for piece in range(3):
            row = piece * exp_count + expert
            part = rest.astype(jnp.bfloat16).astype(jnp.float32)
            share_ref[row : row + 1, 0:token_count] = part
            rest = rest - part
    out_ref[2 * block_len :] = share_ref[...].astype(jnp.bfloat16)
    copies[2].wait()
    copies[3].wait()


def attend_kernel(block_len, scale, *refs):
    place_ref, query_ref, doc_row, *packs = refs[:-4]
    out_ref, marked_ref, keys_ref, values_ref = refs[-4:]
    place = place_ref[0]
    lanes = packs[0].shape[1]
    for i, pack in enumerate(packs):
        rows = pl.ds(pl.multiple_of((place ^ i) * block_len, block_len), block_len)
        keys_ref[rows] = pack[0:block_len]
        values_ref[rows] = pack[block_len : 2 * block_len]
        marked_ref[block_len:, i * lanes : (i + 1) * lanes] = pack[2 * block_len :]
    marked_ref[block_len:, len(packs) * lanes :] = jnp.zeros(
        (marked_ref.shape[0] - block_len, marked_ref.shape[1] - len(packs) * lanes), jnp.bfloat16
    )
    start = pl.multiple_of(place * block_len, block_len)
    query_pos = start + lax.broadcasted_iota(jnp.int32, (block_len, 1), 0)
    key_pos = lax.broadcasted_iota(jnp.int32, doc_row.shape, 1)
    key_doc = doc_row[...]
    query_doc = jnp.sum(jnp.where(query_pos == key_pos, key_doc, 0), axis=1, keepdims=True)
    allowed = (key_pos <= query_pos) & (query_pos - key_pos < WINDOW) & (query_doc == key_doc)
    head_dim = query_ref.shape[2]
    heads = range(query_ref.shape[0])
    scores = [
        lax.dot_general(
            query_ref[head],
            keys_ref[...],
            (((1,), (1,)), ((), ())),
            preferred_element_type=jnp.float32,
        )
        for head in heads
    ]
    scores = [jnp.where(allowed, score * scale, -jnp.inf) for score in scores]
    tops = [jnp.max(score, axis=1, keepdims=True) for score in scores]
    weights = [jnp.exp(score - top) for score, top in zip(scores, tops)]
    inverses = [1.0 / jnp.sum(weight, axis=1, keepdims=True) for weight in weights]
    for head in heads:
        columns = slice(head * head_dim, (head + 1) * head_dim)
        attended = jnp.dot(
            (weights[head] * inverses[head]).astype(jnp.bfloat16),
            values_ref[...],
            preferred_element_type=jnp.float32,
        ).astype(jnp.bfloat16)
        out_ref[:, columns] = attended
        marked_ref[0:block_len, columns] = attended


def rows_of(part, part_width):
    return pl.ds(pl.multiple_of(part * part_width, part_width), part_width)


def near_kernel(place_ref, w_in_hbm, out_ref, sems):
    place = place_ref[0]
    reads = [
        pltpu.make_async_copy(
            w_in_hbm.at[0, rows_of(place ^ j, out_ref.shape[1])], out_ref.at[j], sems.at[j]
        )
        for j in range(out_ref.shape[0])
    ]
    for read in reads:
        read.start()
    for read in reads:
        read.wait()


def experts_kernel(seq_count, group, order, *refs):
    exp_count = len(order)
    place_ref, gain_hbm, w_in_hbm, w_out_hbm, w_near_ref = refs[:5]
    marked = refs[5 : 5 + exp_count]
    refs = refs[5 + exp_count :]
    blocks = {0: marked}
    for d in group:
        if d:
            blocks[d], refs = refs[:exp_count], refs[exp_count:]
    kept, sent, refs = refs[: len(group)], refs[len(group) : 2 * len(group)], refs[2 * len(group) :]
    if 0 in group:
        own_ref, *refs, split_ref = refs
    hidden_ref, share_ref, gain_ref, w_in_ref, w_out_ref, sum_ref, sems = refs
    place = place_ref[0]
    block_len, token_count = marked[0].shape[0] - 16, hidden_ref.shape[1]
    part_width = marked[0].shape[1]
    width = part_width * exp_count
    lanes = 128

    near_count = w_near_ref.shape[0]
    reads = [
        pltpu.make_async_copy(
            w_in_hbm.at[0, rows_of(place ^ j, part_width)], w_in_ref.at[j - near_count], sems.at[j]
        )
        for j in range(near_count, exp_count)
    ]
    depth = hidden_ref.shape[2] // 2
    reads += [
        pltpu.make_async_copy(
            w_out_hbm.at[0, i * depth : (i + 1) * depth],
            w_out_ref.at[i * depth : (i + 1) * depth],
            sems.at[exp_count + i],
        )
        for i in range(2)
    ]
    reads.insert(0, pltpu.make_async_copy(gain_hbm, gain_ref, sems.at[exp_count + 2]))
    for read in reads:
        read.start()

    share_ref[...] = jnp.zeros_like(share_ref)
    for j in range(exp_count):
        share = marked[j][block_len:].astype(jnp.float32)
        row = lax.broadcasted_iota(jnp.int32, share.shape, 0)
        share = jnp.where(row % exp_count == place, share, 0.0)
        share = jnp.sum(share, axis=0, keepdims=True)
        for i, d in enumerate(group):
            line = i * exp_count + order.index(j)
            share_ref[line : line + 1] = share[:, d * lanes : (d + 1) * lanes]
    share = share_ref[...].T
    weight = jnp.concatenate(
        [share[:token_count, i : i + 1] for i in range(len(group) * exp_count)], axis=0
    )

    reads[0].wait()
    squares = [jnp.zeros((block_len, lanes), jnp.float32)] * len(group)
    hidden = None
    for j in range(exp_count):
        source = place ^ j
        gain = gain_ref[source]
        gained = []
        for i, d in enumerate(group):
            value = blocks[d][j][0:block_len].astype(jnp.float32)
            square = value * value
            for start in range(0, part_width, lanes):
                squares[i] = squares[i] + square[:, start : start + lanes]
            gained.append((value * gain).astype(jnp.bfloat16))
            if d == 0:
                split_ref[...] = value.reshape(exp_count, token_count, part_width)
                own_ref[source] = split_ref[place].astype(jnp.bfloat16)
        if j >= near_count:
            reads[1 + j - near_count].wait()
        w_part = w_near_ref[j] if j < near_count else w_in_ref[j - near_count]
        product = jnp.dot(
            jnp.concatenate(gained, axis=0), w_part, preferred_element_type=jnp.float32
        )
        hidden = product if hidden is None else hidden + product
    mean_square = jnp.sum(jnp.concatenate(squares, axis=0), axis=1, keepdims=True) * (1.0 / width)
    hidden = hidden * lax.rsqrt(mean_square + epsilon)
    hidden = hidden * (1.0 / (1.0 + jnp.exp(-hidden)))
    hidden_ref[...] = hidden.reshape(len(group) * exp_count, token_count, hidden.shape[1])
    hidden = jnp.concatenate(
        [hidden_ref[i * exp_count + (place ^ j)] for i in range(len(group)) for j in order], axis=0
    ).astype(jnp.bfloat16)
    half = block_len // 2
    tiles = [slice(start, start + part_width) for start in range(0, width, part_width)]
    reads[1 + exp_count - near_count].wait()
    for columns in tiles:
        sum_ref[:, columns] = jnp.dot(
            hidden[:, :depth], w_out_ref[:depth, columns], preferred_element_type=jnp.float32
        )
    reads[2 + exp_count - near_count].wait()
    for columns in tiles:
        product = sum_ref[:, columns] + jnp.dot(
            hidden[:, depth:], w_out_ref[depth:, columns], preferred_element_type=jnp.float32
        )
        product = (product * weight).astype(jnp.bfloat16)
        for i in range(len(group)):
            low = i * block_len
            kept[i][:, columns] = product[low : low + half]
            sent[i][:, columns] = product[low + half : low + block_len]


def vmem():
    return pl.BlockSpec(memory_space=pltpu.VMEM)


def anywhere():
    return pl.BlockSpec(memory_space=pltpu.HBM)


def gathered_shards(
    queries, keys, values, doc_ids, norm_gain, expert_ids, route_weights, w_in, w_out
):
    block_len, heads_dev, head_dim = queries.shape
    seq_count = lax.axis_size("seq")
    exp_count = lax.axis_size("exp")
    seq_index = lax.axis_index("seq")
    exp_index = lax.axis_index("exp")
    token_count = expert_ids.shape[0]
    part_width = heads_dev * head_dim
    width = part_width * exp_count
    hidden_width = w_in.shape[2]
    half = block_len // 2
    far = range(1, seq_count)

    pack = pl.pallas_call(
        functools.partial(pack_kernel, exp_count),
        out_shape=jax.ShapeDtypeStruct((2 * block_len + 16, head_dim), jnp.bfloat16),
        in_specs=[anywhere()] * 4,
        out_specs=vmem(),
        scratch_shapes=[
            pltpu.VMEM(expert_ids.shape[::-1], jnp.int32),
            pltpu.VMEM(route_weights.shape[::-1], jnp.float32),
            pltpu.VMEM((16, head_dim), jnp.float32),
            pltpu.SemaphoreType.DMA((4,)),
        ],
        compiler_params=pltpu.CompilerParams(vmem_limit_bytes=4 << 20),
        name="pack",
    )(
        *[
            pltpu.with_memory_space_constraint(x, pltpu.HBM)
            for x in (keys[:, 0, :], values[:, 0, :], expert_ids.T, route_weights.T)
        ]
    )
    packs = [pack] + [flipped(pack, "seq", d) for d in far]

    heads, pack = lax.optimization_barrier((jnp.transpose(queries, (1, 0, 2)), pack))
    heads = heads * jnp.bfloat16(0.125)
    w_in_here, _ = lax.optimization_barrier((w_in, pack))
    w_near = pl.pallas_call(
        near_kernel,
        out_shape=pltpu.VMEM((3, part_width, hidden_width), w_in.dtype),
        in_specs=[pl.BlockSpec(memory_space=pltpu.SMEM), anywhere()],
        out_specs=vmem(),
        scratch_shapes=[pltpu.SemaphoreType.DMA((3,))],
        compiler_params=pltpu.CompilerParams(vmem_limit_bytes=4 << 20),
        name="near",
    )(exp_index.reshape(1), pltpu.with_memory_space_constraint(w_in_here, pltpu.HBM))
    heads, w_near = lax.optimization_barrier((heads, w_near))
    packs[0] = pack

    attended, marked = pl.pallas_call(
        functools.partial(attend_kernel, block_len, 8.0 / head_dim**0.5),
        out_shape=[
            jax.ShapeDtypeStruct((block_len, part_width), jnp.bfloat16),
            jax.ShapeDtypeStruct((block_len + 16, part_width), jnp.bfloat16),
        ],
        in_specs=[pl.BlockSpec(memory_space=pltpu.SMEM)] + [vmem()] * (seq_count + 2),
        out_specs=[vmem()] * 2,
        scratch_shapes=[pltpu.VMEM((seq_count * block_len, head_dim), jnp.bfloat16)] * 2,
        compiler_params=pltpu.CompilerParams(vmem_limit_bytes=8 << 20),
        cost_estimate=pl.CostEstimate(
            flops=4 * heads_dev * block_len * seq_count * block_len * head_dim,
            bytes_accessed=1 << 20,
            transcendentals=heads_dev * block_len * seq_count * block_len,
        ),
        name="attend",
    )(seq_index.reshape(1), heads, doc_ids.reshape(1, -1), *packs)

    order = [j for j in range(exp_count) if not j & 1] + [j for j in range(exp_count) if j & 1]
    gain = norm_gain.reshape(exp_count, 1, part_width)
    weights = [pltpu.with_memory_space_constraint(w, pltpu.HBM) for w in (gain, w_in, w_out)]

    def experts(group, last):
        size = len(group)
        operands = list(marked_blocks)
        for d in group:
            if d:
                operands += [there[kind + str(d)] for kind in "zdx"]
                operands.append(there["e" + str(d)] if d != group[0] else last)
        out_shape = [jax.ShapeDtypeStruct((half, width), jnp.bfloat16)] * (2 * size)
        scratch = [
            pltpu.VMEM((size * exp_count, token_count, hidden_width), jnp.float32),
            pltpu.VMEM((head_dim, head_dim), jnp.float32),
            pltpu.VMEM((exp_count, 1, part_width), jnp.float32),
            pltpu.VMEM((exp_count - w_near.shape[0], part_width, hidden_width), jnp.bfloat16),
            pltpu.VMEM((hidden_width, width), jnp.bfloat16),
            pltpu.VMEM((size * block_len, width), jnp.float32),
            pltpu.SemaphoreType.DMA((exp_count + 3,)),
        ]
        if 0 in group:
            split = (exp_count, token_count, part_width)
            out_shape.append(jax.ShapeDtypeStruct(split, jnp.bfloat16))
            scratch.append(pltpu.VMEM(split, jnp.float32))
        in_specs = [pl.BlockSpec(memory_space=pltpu.SMEM)] + [vmem()] * (4 + len(operands))
        in_specs[1:4] = [anywhere()] * 3
        outs = pl.pallas_call(
            functools.partial(experts_kernel, seq_count, group, order),
            out_shape=out_shape,
            in_specs=in_specs,
            out_specs=[vmem()] * len(out_shape),
            scratch_shapes=scratch,
            compiler_params=pltpu.CompilerParams(vmem_limit_bytes=16 << 20),
            cost_estimate=pl.CostEstimate(
                flops=4 * size * block_len * width * hidden_width,
                bytes_accessed=8 << 20,
                transcendentals=size * block_len * hidden_width,
            ),
            name="experts",
        )(exp_index.reshape(1), *weights, w_near, *operands)
        return dict(zip(group, zip(outs[:size], outs[size : 2 * size]))), outs[-1]

    there = {"z0": marked}
    near = {}
    for name in SEQUENCE:
        kind, d = name[0], int(name[1])

        def held(value):
            others = [there[other] for other in WAITS.get(name, ())]
            return lax.optimization_barrier((value, *others))[0] if others else value

        if kind == "z":
            there[name] = flipped(held(attended), "seq", d)
        elif kind in "dx":
            there[name] = flipped(held(there[f"z{d}"]), "exp", 1 if kind == "d" else 2)
        elif kind == "e":
            there[name] = flipped(held(there[f"x{d}"]), "exp", 1)
        elif kind == "g":
            group = GROUPS[d]
            marked_blocks = [there[k + "0"] for k in "zdxe"]
            if group[0]:
                last = held(there[f"e{group[0]}"])
            else:
                last = None
                marked_blocks[3] = held(marked_blocks[3])
            outs, extra = experts(group, last)
            if 0 in group:
                own = extra
            for member, (kept, sent) in outs.items():
                there[f"k{member}"], there[f"s{member}"] = kept, sent
            there[name] = there[f"s{group[0]}"]
        elif kind == "r":
            both = there[f"k{d}"].astype(jnp.float32)
            both = both + flipped(held(there[f"s{d}"]), "exp", 1).astype(jnp.float32)
            near[d], there[name] = both[:token_count], both[token_count:].astype(jnp.bfloat16)
        elif kind == "y":
            there[name] = flipped(held(there[f"r{d}"]), "exp", 2)
            near[d] = near[d] + there[name].astype(jnp.float32)
        elif kind == "w":
            there[name] = flipped(held(near[d].astype(jnp.bfloat16)), "seq", d)
            near[d] = there[name].astype(jnp.float32)
    total = jnp.transpose(own, (1, 0, 2)).reshape(token_count, width).astype(jnp.float32)
    for d in sorted(near, reverse=True):
        total = total + near[d]
    return total.astype(jnp.bfloat16)


def solution(mesh):
    placed = (
        P(("dp", "seq"), "exp", None),
        P(("dp", "seq"), "exp", None),
        P(("dp", "seq"), "exp", None),
        P("dp"),
        P(),
        P(("dp", "seq", "exp"), None),
        P(("dp", "seq", "exp"), None),
        P("exp", None, "seq"),
        P("exp", "seq", None),
    )
    small = mesh.shape["seq"] == 4 and mesh.shape["exp"] == 4
    return jax.shard_map(
        gathered_shards if small else routed_shards,
        mesh=mesh,
        in_specs=placed,
        out_specs=P(("dp", "seq", "exp"), None),
        check_vma=False,
    )
```
